32 devices in a mesh: shard: 16 (over z, y, core), rep: 2 (over x).
Axes of the slice: x: 2, y: 2, z: 4, core: 2. Of those that a mesh axis runs over, the one named last changes fastest.
Arguments:
- entity: float32 [4096, 256], P(('shard', 'rep')), may hold values from -1.5 to 1.5
- rel_weight: float32 [900, 256], replicated, may hold values from -4 to 4
- tile_rel: int32 [1024], P(('shard', 'rep')), may hold values from 0 to 899
- tile_head: int32 [1024], P(('shard', 'rep')), may hold values from 0 to 1
- tile_tail: int32 [1024], P(('shard', 'rep')), may hold values from 0 to 1
- tile_mask: int32 [1024, 128, 128], P(('shard', 'rep')), may hold values 0 or 1
- negatives: int32 [1024, 256], P(('shard', 'rep')), may hold values from 0 to 255
- tile_count: int32 [32], P(('shard', 'rep')), may hold values from 1 to 32, as said below
Outputs:
- entity_grad: float32 [4096, 256], P(('shard', 'rep'))
- rel_grad: float32 [900, 256], replicated
The draws below stay inside these ranges and needn't reach their ends.
Inputs may be any that keep to these rules, and one draw needn't show every extreme that they name: `tile_count`: the used slots of a device are its first ones; some device uses all 32.
All inputs are finite; a program needn't handle non-finite values. No bound on the sum of `tile_mask` on one device may be relied on, other than what follows from the above.
Results may differ from the reference program's by a relative error of at most 0.0003.
Values sent between devices are 32-bit elements; how exact they have to be, the bound alone decides.
No kernel may reach another device: no remote copies, remote signals or barrier semaphores. Data moves between devices by JAX's collectives and lax.ppermute only.
A program may use at most 64 MiB of HBM per device.

```python
import jax
import jax.numpy as jnp
from jax import lax

D = 256
RELS = 900
BLOCK = 128
TILES_DEV = 32
NEG = 256
PART = 256
BLOCKS = 2
ENTITIES = 4096
TILES = 1024
N_SHARD = 16
N_REP = 2


def draw_tile_count(key, part):
    total = N_SHARD * N_REP
    counts = jax.random.randint(jax.random.fold_in(key, 11), (total,), 1, TILES_DEV + 1)
    fullest = jax.random.randint(jax.random.fold_in(key, 12), (), 0, total)
    return counts.at[fullest].set(TILES_DEV).astype(jnp.int32)


def plant(values, stream_key, low, top_value):
    dims = values.shape
    place = [jax.random.randint(jax.random.fold_in(stream_key, axis), (), 0, dims[axis]) for axis in range(len(dims))]
    values = values.at[tuple(place)].set(low)
    longest = dims.index(max(dims))
    place[longest] = (place[longest] + 1) % dims[longest]
    return values.at[tuple(place)].set(top_value)


def shard_levels(rng, shape, shards, least, top_value):
    def one(axis_at, blocks):
        steps = jax.random.uniform(jax.random.fold_in(jax.random.fold_in(rng, 6), axis_at), (blocks,), jnp.float32, least / len(shards), top_value / len(shards))
        return jnp.repeat(jnp.exp(steps), shape[axis_at] // blocks).reshape((-1,) + (1,) * (len(shape) - axis_at - 1))

    level = one(*shards[0])
    for cut in shards[1:]:
        level = level * one(*cut)
    return level


def centred(rng, dims, width, most, shards=(), kind=jnp.bfloat16):
    result = jax.random.normal(rng, dims, jnp.float32) * width
    if len(shards) > 0:
        result = shard_levels(rng, dims, shards, -0.22, 0.18) * result
    return jnp.clip(result, min=-most, max=most).astype(kind)


def setup_inputs(seed: int = 0) -> dict:
    splits = jax.random.split(jax.random.key(seed), 9)
    return {
        "entity": centred(splits[0], (ENTITIES, D), 0.25, 1.5, ((0, 32),), jnp.float32),
        "rel_weight": centred(splits[1], (RELS, D), 1.0, 4.0, (), jnp.float32),
        "tile_rel": plant(jax.random.randint(splits[2], (TILES,), 0, RELS), jax.random.fold_in(splits[2], 1), 0, RELS - 1).astype(jnp.int32),
        "tile_head": plant(jax.random.randint(splits[3], (TILES,), 0, BLOCKS), jax.random.fold_in(splits[3], 1), 0, BLOCKS - 1).astype(jnp.int32),
        "tile_tail": plant(jax.random.randint(splits[4], (TILES,), 0, BLOCKS), jax.random.fold_in(splits[4], 1), 0, BLOCKS - 1).astype(jnp.int32),
        "tile_mask": plant((jax.random.randint(splits[5], (TILES, BLOCK, BLOCK), 0, 16) < 1).astype(jnp.int32), jax.random.fold_in(splits[5], 1), 0, 1),
        "negatives": plant(jax.random.randint(splits[6], (TILES, NEG), 0, PART), jax.random.fold_in(splits[6], 1), 0, PART - 1).astype(jnp.int32),
        "tile_count": draw_tile_count(jax.random.fold_in(splits[8], 71), 0),
    }


def device_terms(head, tail, rel_weight, rels, heads, tails, masks, negs, count):
    high = lax.Precision.HIGHEST
    blocks = head.shape[0] // BLOCK
    head_b = head.reshape(blocks, BLOCK, D)
    tail_b = tail.reshape(blocks, BLOCK, D)
    hrows = head_b[heads]
    trows = tail_b[tails]
    weights = rel_weight[rels]
    nrows = tail[negs]
    live = (jnp.arange(rels.shape[0], dtype=jnp.int32) < count).astype(jnp.float32)
    scaled = hrows * weights[:, None, :]
    scores = jnp.einsum("tik,tjk->tij", scaled, trows, precision=high)
    grads = -(masks.astype(jnp.float32) * live[:, None, None]) * jax.nn.sigmoid(-scores)
    negsc = jnp.einsum("tik,tjk->tij", scaled, nrows, precision=high)
    ngrads = live[:, None, None] * jax.nn.sigmoid(negsc)
    mixed = jnp.einsum("tij,tjk->tik", grads, trows, precision=high) + jnp.einsum("tij,tjk->tik", ngrads, nrows, precision=high)
    dhead = mixed * weights[:, None, :]
    dtail = jnp.einsum("tij,tik->tjk", grads, scaled, precision=high)
    dneg = jnp.einsum("tij,tik->tjk", ngrads, scaled, precision=high)
    dweight = jnp.sum(hrows * mixed, axis=1)
    head_grad = jnp.zeros((blocks, BLOCK, D), jnp.float32).at[heads].add(dhead).reshape(-1, D)
    tail_grad = jnp.zeros((blocks, BLOCK, D), jnp.float32).at[tails].add(dtail).reshape(-1, D)
    tail_grad = tail_grad.at[negs.reshape(-1)].add(dneg.reshape(-1, D))
    rel_grad = jnp.zeros((RELS, D), jnp.float32).at[rels].add(dweight)
    return head_grad, tail_grad, rel_grad


def reference(entity, rel_weight, tile_rel, tile_head, tile_tail, tile_mask, negatives, tile_count):
    parts = entity.reshape(N_SHARD, PART, D)
    rels = tile_rel.reshape(N_SHARD, N_REP, TILES_DEV)
    heads = tile_head.reshape(N_SHARD, N_REP, TILES_DEV)
    tails = tile_tail.reshape(N_SHARD, N_REP, TILES_DEV)
    masks = tile_mask.reshape(N_SHARD, N_REP, TILES_DEV, BLOCK, BLOCK)
    negs = negatives.reshape(N_SHARD, N_REP, TILES_DEV, NEG)
    counts = tile_count.reshape(N_SHARD, N_REP)

    def per_shard(carry, index):
        grads, rel_total = carry
        lower = (index + N_SHARD - 1) % N_SHARD
        head = parts[index]
        tail = parts[lower]
        terms = jax.vmap(lambda a, b, c, m, n, k: device_terms(head, tail, rel_weight, a, b, c, m, n, k))(
            rels[index], heads[index], tails[index], masks[index], negs[index], counts[index])
        grads = grads.at[index].add(jnp.sum(terms[0], axis=0))
        grads = grads.at[lower].add(jnp.sum(terms[1], axis=0))
        rel_total = rel_total + jnp.sum(terms[2], axis=0)
        return (grads, rel_total), None

    start = (jnp.zeros((N_SHARD, PART, D), jnp.float32), jnp.zeros((RELS, D), jnp.float32))
    (grads, rel_total), unused = lax.scan(per_shard, start, jnp.arange(N_SHARD, dtype=jnp.int32))
    return grads.reshape(ENTITIES, D), rel_total
```

```python
import functools

import jax
import jax.numpy as jnp
from jax import lax
from jax.experimental import pallas as pl
from jax.experimental.pallas import tpu as pltpu
from jax.sharding import PartitionSpec as P

AXES = ("shard", "rep")
F32 = jnp.float32
BF16 = jnp.bfloat16
GROUP = 8
LANES = 128
SUBLANES = 8
VMEM_BYTES = 32 * 1024 * 1024


def halves(value):
    high = value.astype(BF16)
    low = (value - high.astype(F32)).astype(BF16)
    return high, low


def dot3(left, right, dims):
    product = functools.partial(lax.dot_general, dimension_numbers=(dims, ((), ())), preferred_element_type=F32)
    return product(left[0], right[0]) + (product(left[0], right[1]) + product(left[1], right[0]))


def prepare_kernel(rel_ids, count, negatives, rel_weight, counts_out, weights_out):
    tiles, partition = counts_out.shape
    draws = negatives.shape[1]
    for tile in range(tiles):
        weights_out[tile : tile + 1, :] = rel_weight[pl.ds(rel_ids[tile], 1), :]
    chosen = negatives[...]
    columns = lax.broadcasted_iota(jnp.int32, (tiles, partition), 1)
    total = jnp.zeros((tiles, partition), F32)
    for draw in range(draws):
        total = total + jnp.where(chosen[:, draw : draw + 1] == columns, 1.0, 0.0)
    slots = lax.broadcasted_iota(jnp.int32, (tiles, partition), 0)
    counts_out[...] = jnp.where(slots < count[0], total, 0.0)


def tiles_kernel(blocks, *refs):
    head_ids, tail_ids, count, place = refs[:4]
    head_in = refs[4 : 4 + blocks]
    tail_in = refs[4 + blocks : 4 + 2 * blocks]
    mask, counts, weights, names = refs[4 + 2 * blocks : 8 + 2 * blocks]
    terms = refs[8 + 2 * blocks]
    head_out = refs[9 + 2 * blocks : 9 + 3 * blocks]
    tail_out = refs[9 + 3 * blocks : 9 + 4 * blocks]
    heads, tails, head_grad, tail_grad = refs[9 + 4 * blocks :]
    tiles, block, _ = mask.shape
    width = weights.shape[1]
    mine = place[0]
    for k in range(blocks):
        heads[mine ^ k] = head_in[k][...]
        tails[mine ^ k] = tail_in[k][...]
    head_grad[...] = jnp.zeros_like(head_grad)
    tail_grad[...] = jnp.zeros_like(tail_grad)
    terms[2 * tiles :, :] = jnp.zeros((terms.shape[0] - 2 * tiles, LANES), F32)
    terms[2 * tiles : 2 * tiles + 1, :] = names[...]
    tail_pair = halves(tails[...].reshape(blocks * block, width))

    def step(index, carry):
        base = pl.multiple_of(index * GROUP, GROUP)
        slots = [base + u for u in range(GROUP)]
        rows = [heads[head_ids[slot]] for slot in slots]
        scales = weights[pl.ds(base, GROUP), :]
        scales = [scales[u : u + 1, :] for u in range(GROUP)]
        repeats = counts[pl.ds(base, GROUP), :]
        scaled = halves(jnp.concatenate([a * b for a, b in zip(rows, scales)], axis=0))
        scores = dot3(scaled, tail_pair, ((1,), (1,)))
        grads = []
        for u, slot in enumerate(slots):
            adjacent = mask[slot].astype(F32)
            live = slot < count[0]
            parts = []
            for b in range(blocks):
                flag = jnp.where(jnp.logical_and(live, tail_ids[slot] == b), 1.0, 0.0)
                times = repeats[u : u + 1, b * block : (b + 1) * block]
                score = scores[u * block : (u + 1) * block, b * block : (b + 1) * block]
                odds = jnp.exp(jnp.minimum(-score, 80.0))
                parts.append((times - (adjacent * flag) * odds) / (1.0 + odds))
            grads.append(jnp.concatenate(parts, axis=1))
        grads = halves(jnp.concatenate(grads, axis=0))
        mixed = dot3(grads, tail_pair, ((1,), (0,)))
        sums = []
        for u, slot in enumerate(slots):
            part = mixed[u * block : (u + 1) * block, :]
            sums.append(jnp.sum(rows[u] * part, axis=0, keepdims=True))
            head_grad[head_ids[slot]] += part * scales[u]
        sums = jnp.concatenate(sums, axis=0)
        terms[pl.ds(base, GROUP), :] = sums[:, :LANES]
        terms[pl.ds(tiles + base, GROUP), :] = sums[:, LANES:]
        tail_grad[...] += dot3(grads, scaled, ((0,), (0,))).reshape(tail_grad.shape)
        return carry

    lax.fori_loop(0, tiles // GROUP, step, 0)
    for k in range(blocks):
        head_out[k][...] = head_grad[mine ^ k]
        tail_out[k][...] = tail_grad[mine ^ k]


def combine_kernel(gathered, out):
    devices = gathered.shape[0]
    tiles = (gathered.shape[1] - SUBLANES) // 2
    rels, width = out.shape
    padded = -(-rels // SUBLANES) * SUBLANES
    share = LANES // tiles
    lanes = lax.broadcasted_iota(jnp.int32, (1, LANES), 1) // tiles
    rows = lax.broadcasted_iota(jnp.int32, (padded, LANES), 0)
    hits = []
    for first in range(0, devices, share):
        names = gathered[first, 2 * tiles : 2 * tiles + 1, :]
        for other in range(1, share):
            names = jnp.where(lanes == other, gathered[first + other, 2 * tiles : 2 * tiles + 1, :], names)
        hits.append(jnp.where(rows == names.astype(jnp.int32), 1.0, 0.0).astype(BF16))
    hits = jnp.concatenate(hits, axis=1)
    left = gathered[:, :tiles, :].reshape(devices * tiles, LANES)
    right = gathered[:, tiles : 2 * tiles, :].reshape(devices * tiles, LANES)
    high, low = halves(jnp.concatenate([left, right], axis=1))
    total = jnp.dot(hits, high, preferred_element_type=F32) + jnp.dot(hits, low, preferred_element_type=F32)

    @pl.when(pl.program_id(0) == 0)
    def _():
        out[...] = total[:rels]

    @pl.when(pl.program_id(0) != 0)
    def _():
        out[...] += total[:rels]


def spec(space):
    return pl.BlockSpec(memory_space=space)


def permute(value, shards, reps, shift, flip):
    route = [
        (s * reps + r, (s + shift) % shards * reps + (r ^ flip)) for s in range(shards) for r in range(reps)
    ]
    return lax.ppermute(value, AXES, route)


def gather_all(value, shards, reps):
    total = shards * reps
    low = reps.bit_length() - 1
    top = total.bit_length() - 1
    order = list(range(top - 1, low, -1)) + list(range(low - 1, -1, -1)) + [low]
    index = lax.axis_index("shard") * reps + lax.axis_index("rep")
    held = value[None]
    while order:
        bits, order = order[:2], order[2:]
        ways = 1 << len(bits)
        parts = [held]
        code = sum(((index >> bit) & 1) << i for i, bit in enumerate(bits))
        for k in range(1, ways):
            flip = sum(((k >> i) & 1) << bit for i, bit in enumerate(bits))
            parts.append(lax.ppermute(held, AXES, [(d, d ^ flip) for d in range(total)]))
        for i in range(len(bits)):
            swap = ((code >> i) & 1) == 1
            swapped = [parts[k ^ (1 << i)] for k in range(ways)]
            parts = [jnp.where(swap, b, a) for a, b in zip(parts, swapped)]
        held = jnp.concatenate(parts, axis=0)
    return held


def local(shards, reps, entity, rel_weight, tile_rel, tile_head, tile_tail, tile_mask, negatives, tile_count):
    tiles = tile_rel.shape[0]
    block, width = entity.shape
    rels = rel_weight.shape[0]
    partition = block * reps
    smem, vmem = spec(pltpu.SMEM), spec(pltpu.VMEM)
    params = pltpu.CompilerParams(vmem_limit_bytes=VMEM_BYTES)

    heads = [entity] + [permute(entity, shards, reps, 0, k) for k in range(1, reps)]
    tails = [permute(entity, shards, reps, 1, k) for k in range(reps)]
    counts, weights = pl.pallas_call(
        prepare_kernel,
        out_shape=(
            jax.ShapeDtypeStruct((tiles, partition), F32),
            jax.ShapeDtypeStruct((tiles, width), F32),
        ),
        in_specs=[smem, smem, vmem, vmem],
        out_specs=(vmem, vmem),
        compiler_params=params,
        cost_estimate=pl.CostEstimate(flops=2 * tiles * partition * 256, bytes_accessed=1 << 20, transcendentals=0),
        name="prepare",
    )(tile_rel, tile_count, negatives, rel_weight)
    names = jnp.tile(tile_rel.astype(F32), LANES // tiles)[None]
    place = lax.axis_index("rep").astype(jnp.int32)[None]
    piece = jax.ShapeDtypeStruct((block, width), F32)
    results = pl.pallas_call(
        functools.partial(tiles_kernel, reps),
        out_shape=[jax.ShapeDtypeStruct((2 * tiles + SUBLANES, LANES), F32)] + [piece] * (2 * reps),
        in_specs=[smem] * 4 + [vmem] * (2 * reps + 4),
        out_specs=[vmem] * (2 * reps + 1),
        scratch_shapes=[pltpu.VMEM((reps, block, width), F32)] * 4,
        compiler_params=params,
        cost_estimate=pl.CostEstimate(
            flops=18 * tiles * block * partition * width, bytes_accessed=4 << 20, transcendentals=0
        ),
        name="tiles",
    )(tile_head, tile_tail, tile_count, place, *heads, *tails, tile_mask, counts, weights, names)
    terms, head_parts, tail_parts = results[0], results[1 : 1 + reps], results[1 + reps :]

    gathered = gather_all(terms, shards, reps)
    entity_grad = head_parts[0]
    for k in range(1, reps):
        entity_grad = entity_grad + permute(head_parts[k], shards, reps, 0, k)
    for k in range(reps):
        entity_grad = entity_grad + permute(tail_parts[k], shards, reps, -1, k)

    batch = 32
    rel_grad = pl.pallas_call(
        combine_kernel,
        out_shape=jax.ShapeDtypeStruct((rels, width), F32),
        grid=(shards * reps // batch,),
        in_specs=[pl.BlockSpec((batch,) + gathered.shape[1:], lambda i: (i, 0, 0))],
        out_specs=pl.BlockSpec((rels, width), lambda i: (0, 0)),
        compiler_params=params,
        cost_estimate=pl.CostEstimate(
            flops=4 * rels * shards * reps * tiles * width, bytes_accessed=2 << 20, transcendentals=0
        ),
        name="combine",
    )(gathered)
    return (entity_grad, rel_grad)


def solution(mesh):
    sizes = dict(mesh.shape)
    return jax.shard_map(
        functools.partial(local, sizes["shard"], sizes["rep"]),
        mesh=mesh,
        in_specs=(
            P(AXES, None),
            P(),
            P(AXES),
            P(AXES),
            P(AXES),
            P(AXES, None, None),
            P(AXES, None),
            P(AXES),
        ),
        out_specs=(P(AXES, None), P()),
        check_vma=False,
    )
```

```python
import functools

import jax
import jax.numpy as jnp
from jax import lax
from jax.experimental import pallas as pl
from jax.experimental.pallas import tpu as pltpu
from jax.sharding import PartitionSpec as P

AXES = ("shard", "rep")
F32 = jnp.float32
BF16 = jnp.bfloat16
GROUP = 8
LANES = 128
SUBLANES = 8
VMEM_BYTES = 40 * 1024 * 1024
LOG2E = 1.4426950408889634


def halves(value):
    high = value.astype(BF16)
    low = (value - high.astype(F32)).astype(BF16)
    return high, low


def stacked_left(pair, axis):
    return jnp.concatenate([pair[0], pair[0], pair[1]], axis=axis)


def stacked_right(pair, axis):
    return jnp.concatenate([pair[0], pair[1], pair[0]], axis=axis)


def dot(left, right, left_axis, right_axis):
    return lax.dot_general(
        left,
        right,
        dimension_numbers=(((left_axis,), (right_axis,)), ((), ())),
        preferred_element_type=F32,
    )


def prepare_kernel(count, rel_ids, negatives, rel_weight, entity, *refs):
    counts_out, weights_out, names_out, entity_out = refs[:4]
    ids, draws, table, sems = refs[4:]
    tiles, partition = counts_out.shape
    copies = [
        pltpu.make_async_copy(source, target, sems.at[i])
        for i, (source, target) in enumerate(
            [(rel_ids, ids), (negatives, draws), (rel_weight, table), (entity, entity_out)]
        )
    ]
    for copy in copies:
        copy.start()
    copies[1].wait()
    chosen = draws[...]
    columns = lax.broadcasted_iota(jnp.int32, (tiles, partition), 1)
    total = jnp.zeros((tiles, partition), F32)
    for draw in range(chosen.shape[1]):
        total = total + jnp.where(chosen[:, draw : draw + 1] == columns, 1.0, 0.0)
    slots = lax.broadcasted_iota(jnp.int32, (tiles, partition), 0)
    counts_out[...] = jnp.where(slots < count[0], total, 0.0)
    copies[0].wait()
    copies[2].wait()
    lanes = lax.broadcasted_iota(jnp.int32, (1, LANES), 1) % tiles
    names = jnp.zeros((1, LANES), jnp.int32)
    for tile in range(tiles):
        weights_out[tile : tile + 1, :] = table[pl.ds(ids[tile], 1), :]
        names = jnp.where(lanes == tile, ids[tile], names)
    names_out[...] = names.astype(F32)
    copies[3].wait()


def tiles_kernel(blocks, *refs):
    count, place, head_in_ids, tail_in_ids = refs[:4]
    head_in = refs[4 : 4 + blocks]
    tail_in = refs[4 + blocks : 4 + 2 * blocks]
    mask, counts, weights, names = refs[4 + 2 * blocks : 8 + 2 * blocks]
    terms = refs[8 + 2 * blocks]
    head_out, tail_out = refs[9 + 2 * blocks : 11 + 2 * blocks]
    heads, tails, head_grad, tail_grad, head_ids, tail_ids, sems = refs[11 + 2 * blocks :]
    tiles, block, _ = mask.shape
    width = weights.shape[1]
    mine = place[0]
    copies = [
        pltpu.make_async_copy(head_in_ids, head_ids, sems.at[0]),
        pltpu.make_async_copy(tail_in_ids, tail_ids, sems.at[1]),
    ]
    for copy in copies:
        copy.start()
    for k in range(blocks):
        heads[mine ^ k] = head_in[k][...]
        tails[mine ^ k] = tail_in[k][...]
    head_grad[...] = jnp.zeros_like(head_grad)
    terms[2 * tiles :, :] = jnp.zeros((terms.shape[0] - 2 * tiles, LANES), F32)
    terms[2 * tiles : 2 * tiles + 1, :] = names[...]
    tail = tails[...].reshape(blocks * block, width)
    for_scores = stacked_right(halves(tail * -LOG2E), 1)
    for_mixed = stacked_right(halves(tail), 0)
    for copy in copies:
        copy.wait()

    for base in range(0, tiles, GROUP):
        slots = range(base, base + GROUP)
        rows = [heads[head_ids[slot]] for slot in slots]
        scales = [weights[slot : slot + 1, :] for slot in slots]
        scaled = halves(jnp.concatenate([a * b for a, b in zip(rows, scales)], axis=0))
        scores = dot(stacked_left(scaled, 1), for_scores, 1, 1)
        grads = []
        for u, slot in enumerate(slots):
            adjacent = mask[slot]
            live = slot < count[0]
            parts = []
            for b in range(blocks):
                flag = jnp.where(jnp.logical_and(live, tail_ids[slot] == b), 1.0, 0.0)
                times = counts[slot : slot + 1, b * block : (b + 1) * block]
                score = scores[u * block : (u + 1) * block, b * block : (b + 1) * block]
                odds = jnp.exp2(jnp.minimum(score, 115.0))
                parts.append((times - (adjacent * flag) * odds) / (1.0 + odds))
            grads.append(jnp.concatenate(parts, axis=1))
        grads = halves(jnp.concatenate(grads, axis=0))
        mixed = dot(stacked_left(grads, 1), for_mixed, 1, 0)
        for u, slot in enumerate(slots):
            part = mixed[u * block : (u + 1) * block, :]
            term = jnp.sum(rows[u] * part, axis=0, keepdims=True)
            terms[slot : slot + 1, :] = term[:, :LANES]
            terms[tiles + slot : tiles + slot + 1, :] = term[:, LANES:]
            head_grad[head_ids[slot]] += part * scales[u]
        tail_part = dot(stacked_left(grads, 0), stacked_right(scaled, 0), 0, 0).reshape(tail_grad.shape)
        if base == 0:
            tail_grad[...] = tail_part
        else:
            tail_grad[...] += tail_part

    for k in range(blocks):
        head_out[k] = head_grad[mine ^ k]
        tail_out[k] = tail_grad[mine ^ k]


def combine_kernel(gathered, before, out):
    devices = gathered.shape[0]
    tiles = (gathered.shape[1] - SUBLANES) // 2
    rels, width = out.shape
    padded = -(-rels // SUBLANES) * SUBLANES
    share = LANES // tiles
    lanes = lax.broadcasted_iota(jnp.int32, (1, LANES), 1) // tiles
    rows = lax.broadcasted_iota(jnp.int32, (padded, LANES), 0)
    hits = []
    for first in range(0, devices, share):
        names = gathered[first, 2 * tiles : 2 * tiles + 1, :]
        for other in range(1, share):
            names = jnp.where(lanes == other, gathered[first + other, 2 * tiles : 2 * tiles + 1, :], names)
        hits.append(jnp.where(rows == names.astype(jnp.int32), 1.0, 0.0).astype(BF16))
    hits = jnp.concatenate(hits, axis=1)
    left = gathered[:, :tiles, :].reshape(devices * tiles, LANES)
    right = gathered[:, tiles : 2 * tiles, :].reshape(devices * tiles, LANES)
    high, low = halves(jnp.concatenate([left, right], axis=1))
    total = jnp.dot(hits, high, preferred_element_type=F32) + jnp.dot(hits, low, preferred_element_type=F32)

    @pl.when(pl.program_id(0) == 0)
    def _():
        if before is None:
            out[...] = total[:rels]
        else:
            out[...] = before[...] + total[:rels]

    @pl.when(pl.program_id(0) != 0)
    def _():
        out[...] += total[:rels]


def combine(gathered, rels, width, before=None):
    batch = min(gathered.shape[0], 32)
    whole = pl.BlockSpec((rels, width), lambda i: (0, 0))
    kernel = combine_kernel
    operands, in_specs = [gathered], [pl.BlockSpec((batch,) + gathered.shape[1:], lambda i: (i, 0, 0))]
    if before is None:
        kernel = lambda held, out: combine_kernel(held, None, out)
    else:
        operands.append(before)
        in_specs.append(whole)
    return pl.pallas_call(
        kernel,
        out_shape=jax.ShapeDtypeStruct((rels, width), F32),
        grid=(gathered.shape[0] // batch,),
        in_specs=in_specs,
        out_specs=whole,
        compiler_params=pltpu.CompilerParams(vmem_limit_bytes=VMEM_BYTES),
        cost_estimate=pl.CostEstimate(
            flops=4 * rels * gathered.shape[0] * 32 * width, bytes_accessed=2 << 20, transcendentals=0
        ),
        name="combine",
    )(*operands)


def spec(space):
    return pl.BlockSpec(memory_space=space)


def permute(value, shards, reps, shift, flip):
    route = [
        (s * reps + r, (s + shift) % shards * reps + (r ^ flip)) for s in range(shards) for r in range(reps)
    ]
    return lax.ppermute(value, AXES, route)


def exchange(held, bits, index, total):
    ways = 1 << len(bits)
    parts = [held]
    code = sum(((index >> bit) & 1) << i for i, bit in enumerate(bits))
    for k in range(1, ways):
        flip = sum(((k >> i) & 1) << bit for i, bit in enumerate(bits))
        parts.append(lax.ppermute(held, AXES, [(d, d ^ flip) for d in range(total)]))
    for i in range(len(bits)):
        swap = ((code >> i) & 1) == 1
        swapped = [parts[k ^ (1 << i)] for k in range(ways)]
        parts = [jnp.where(swap, b, a) for a, b in zip(parts, swapped)]
    return jnp.concatenate(parts, axis=0)


def local(shards, reps, entity, rel_weight, tile_rel, tile_head, tile_tail, tile_mask, negatives, tile_count):
    tiles = tile_rel.shape[0]
    block, width = entity.shape
    rels = rel_weight.shape[0]
    partition = block * reps
    smem, vmem = spec(pltpu.SMEM), spec(pltpu.VMEM)
    params = pltpu.CompilerParams(vmem_limit_bytes=VMEM_BYTES)

    others = [permute(entity, shards, reps, 0, k) for k in range(1, reps)]
    tails = [permute(entity, shards, reps, 1, k) for k in range(reps)]
    counts, weights, names, own = pl.pallas_call(
        prepare_kernel,
        out_shape=(
            jax.ShapeDtypeStruct((tiles, partition), F32),
            jax.ShapeDtypeStruct((tiles, width), F32),
            jax.ShapeDtypeStruct((1, LANES), F32),
            jax.ShapeDtypeStruct(entity.shape, F32),
        ),
        in_specs=[smem] + [spec(pl.ANY)] * 4,
        out_specs=(vmem, vmem, vmem, vmem),
        scratch_shapes=[
            pltpu.SMEM(tile_rel.shape, jnp.int32),
            pltpu.VMEM(negatives.shape, jnp.int32),
            pltpu.VMEM(rel_weight.shape, F32),
            pltpu.SemaphoreType.DMA((4,)),
        ],
        compiler_params=params,
        cost_estimate=pl.CostEstimate(flops=2 * tiles * partition * 256, bytes_accessed=4 << 20, transcendentals=0),
        name="prepare",
    )(tile_count, tile_rel, negatives, rel_weight, entity)
    mask = tile_mask.astype(F32)
    place = lax.axis_index("rep").astype(jnp.int32)[None]
    pieces = jax.ShapeDtypeStruct((reps, block, width), F32)
    terms, head_parts, tail_parts = pl.pallas_call(
        functools.partial(tiles_kernel, reps),
        out_shape=[jax.ShapeDtypeStruct((2 * tiles + SUBLANES, LANES), F32), pieces, pieces],
        in_specs=[smem] * 2 + [spec(pl.ANY)] * 2 + [vmem] * (2 * reps + 4),
        out_specs=[vmem] * 3,
        scratch_shapes=[pltpu.VMEM((reps, block, width), F32)] * 4
        + [pltpu.SMEM((tiles,), jnp.int32)] * 2
        + [pltpu.SemaphoreType.DMA((2,))],
        compiler_params=params,
        cost_estimate=pl.CostEstimate(
            flops=18 * tiles * block * partition * width, bytes_accessed=4 << 20, transcendentals=0
        ),
        name="tiles",
    )(tile_count, place, tile_head, tile_tail, own, *others, *tails, mask, counts, weights, names)

    total = shards * reps
    low = reps.bit_length() - 1
    top = total.bit_length() - 1
    order = list(range(top - 1, low, -1)) + list(range(low - 1, -1, -1))
    index = lax.axis_index("shard") * reps + lax.axis_index("rep")
    returned = permute(tail_parts, shards, reps, -1, 0)
    held = exchange(terms[None], order[:2], index, total)
    for i in range(2, len(order), 2):
        held = exchange(held, order[i : i + 2], index, total)
    held, returned = lax.optimization_barrier((held, returned))
    theirs = lax.ppermute(held, AXES, [(d, d ^ (1 << low)) for d in range(total)])
    entity_grad = head_parts[0] + returned[0]
    for k in range(1, reps):
        entity_grad = entity_grad + permute(head_parts[k] + returned[k], shards, reps, 0, k)
    half = combine(held, rels, width)
    rel_grad = combine(theirs, rels, width, half)
    return (entity_grad, rel_grad)


def solution(mesh):
    sizes = dict(mesh.shape)
    return jax.shard_map(
        functools.partial(local, sizes["shard"], sizes["rep"]),
        mesh=mesh,
        in_specs=(
            P(AXES, None),
            P(),
            P(AXES),
            P(AXES),
            P(AXES),
            P(AXES, None, None),
            P(AXES, None),
            P(AXES),
        ),
        out_specs=(P(AXES, None), P()),
        check_vma=False,
    )
```

```python
import functools

import jax
import jax.numpy as jnp
from jax import lax
from jax.experimental import pallas as pl
from jax.experimental.pallas import tpu as pltpu
from jax.sharding import PartitionSpec as P

AXES = ("shard", "rep")
F32 = jnp.float32
BF16 = jnp.bfloat16
GROUP = 8
LANES = 128
SUBLANES = 8
VMEM_BYTES = 40 * 1024 * 1024
LOG2E = 1.4426950408889634


def halves(value):
    high = value.astype(BF16)
    low = (value - high.astype(F32)).astype(BF16)
    return high, low


def stacked_left(pair, axis):
    return jnp.concatenate([pair[0], pair[0], pair[1]], axis=axis)


def stacked_right(pair, axis):
    return jnp.concatenate([pair[0], pair[1], pair[0]], axis=axis)


def dot(left, right, left_axis, right_axis):
    return lax.dot_general(
        left,
        right,
        dimension_numbers=(((left_axis,), (right_axis,)), ((), ())),
        preferred_element_type=F32,
    )


def prepare_kernel(count, rel_ids, negatives, rel_weight, entity, *refs):
    counts_out, weights_out, names_out, entity_out = refs[:4]
    ids, draws, table, sems = refs[4:]
    tiles, partition = counts_out.shape
    copies = [
        pltpu.make_async_copy(source, target, sems.at[i])
        for i, (source, target) in enumerate(
            [(rel_ids, ids), (negatives, draws), (rel_weight, table), (entity, entity_out)]
        )
    ]
    for copy in copies:
        copy.start()
    copies[1].wait()
    chosen = draws[...]
    columns = lax.broadcasted_iota(jnp.int32, (tiles, partition), 1)
    total = jnp.zeros((tiles, partition), F32)
    for draw in range(chosen.shape[1]):
        total = total + jnp.where(chosen[:, draw : draw + 1] == columns, 1.0, 0.0)
    slots = lax.broadcasted_iota(jnp.int32, (tiles, partition), 0)
    counts_out[...] = jnp.where(slots < count[0], total, 0.0)
    copies[0].wait()
    copies[2].wait()
    lanes = lax.broadcasted_iota(jnp.int32, (1, LANES), 1) % tiles
    names = jnp.zeros((1, LANES), jnp.int32)
    for tile in range(tiles):
        weights_out[tile : tile + 1, :] = table[pl.ds(ids[tile], 1), :]
        names = jnp.where(lanes == tile, ids[tile], names)
    names_out[...] = names.astype(F32)
    copies[3].wait()


def tiles_kernel(blocks, *refs):
    count, place, head_in_ids, tail_in_ids = refs[:4]
    head_in = refs[4 : 4 + blocks]
    tail_in = refs[4 + blocks : 4 + 2 * blocks]
    mask, counts, weights, names = refs[4 + 2 * blocks : 8 + 2 * blocks]
    terms = refs[8 + 2 * blocks]
    head_out, tail_out = refs[9 + 2 * blocks : 11 + 2 * blocks]
    heads, tails, head_grad, tail_grad, head_ids, tail_ids, sems = refs[11 + 2 * blocks :]
    tiles, block, _ = mask.shape
    width = weights.shape[1]
    mine = place[0]
    copies = [
        pltpu.make_async_copy(head_in_ids, head_ids, sems.at[0]),
        pltpu.make_async_copy(tail_in_ids, tail_ids, sems.at[1]),
    ]
    for copy in copies:
        copy.start()
    for k in range(blocks):
        heads[mine ^ k] = head_in[k][...]
        tails[mine ^ k] = tail_in[k][...]
    head_grad[...] = jnp.zeros_like(head_grad)
    terms[2 * tiles :, :] = jnp.zeros((terms.shape[0] - 2 * tiles, LANES), F32)
    terms[2 * tiles : 2 * tiles + 1, :] = names[...]
    tail = tails[...].reshape(blocks * block, width)
    for_scores = stacked_right(halves(tail * -LOG2E), 1)
    for_mixed = stacked_right(halves(tail), 0)
    for copy in copies:
        copy.wait()

    for base in range(0, tiles, GROUP):
        slots = range(base, base + GROUP)
        rows = [heads[head_ids[slot]] for slot in slots]
        scales = [weights[slot : slot + 1, :] for slot in slots]
        scaled = halves(jnp.concatenate([a * b for a, b in zip(rows, scales)], axis=0))
        scores = dot(stacked_left(scaled, 1), for_scores, 1, 1)
        grads = []
        for u, slot in enumerate(slots):
            adjacent = mask[slot]
            live = slot < count[0]
            parts = []
            for b in range(blocks):
                flag = jnp.where(jnp.logical_and(live, tail_ids[slot] == b), 1.0, 0.0)
                times = counts[slot : slot + 1, b * block : (b + 1) * block]
                score = scores[u * block : (u + 1) * block, b * block : (b + 1) * block]
                odds = jnp.exp2(jnp.minimum(score, 115.0))
                parts.append((times - (adjacent * flag) * odds) / (1.0 + odds))
            grads.append(jnp.concatenate(parts, axis=1))
        grads = halves(jnp.concatenate(grads, axis=0))
        mixed = dot(stacked_left(grads, 1), for_mixed, 1, 0)
        for u, slot in enumerate(slots):
            part = mixed[u * block : (u + 1) * block, :]
            term = jnp.sum(rows[u] * part, axis=0, keepdims=True)
            terms[slot : slot + 1, :] = term[:, :LANES]
            terms[tiles + slot : tiles + slot + 1, :] = term[:, LANES:]
            head_grad[head_ids[slot]] += part * scales[u]
        tail_part = dot(stacked_left(grads, 0), stacked_right(scaled, 0), 0, 0).reshape(tail_grad.shape)
        if base == 0:
            tail_grad[...] = tail_part
        else:
            tail_grad[...] += tail_part

    for k in range(blocks):
        head_out[k] = head_grad[mine ^ k]
        tail_out[k] = tail_grad[mine ^ k]


def combine_kernel(gathered, before, out):
    devices = gathered.shape[0]
    tiles = (gathered.shape[1] - SUBLANES) // 2
    rels, width = out.shape
    padded = -(-rels // SUBLANES) * SUBLANES
    share = LANES // tiles
    lanes = lax.broadcasted_iota(jnp.int32, (1, LANES), 1) // tiles
    rows = lax.broadcasted_iota(jnp.int32, (padded, LANES), 0)
    hits = []
    for first in range(0, devices, share):
        names = gathered[first, 2 * tiles : 2 * tiles + 1, :]
        for other in range(1, share):
            names = jnp.where(lanes == other, gathered[first + other, 2 * tiles : 2 * tiles + 1, :], names)
        hits.append(jnp.where(rows == names.astype(jnp.int32), 1.0, 0.0).astype(BF16))
    hits = jnp.concatenate(hits, axis=1)
    left = gathered[:, :tiles, :].reshape(devices * tiles, LANES)
    right = gathered[:, tiles : 2 * tiles, :].reshape(devices * tiles, LANES)
    high, low = halves(jnp.concatenate([left, right], axis=1))
    total = jnp.dot(hits, high, preferred_element_type=F32) + jnp.dot(hits, low, preferred_element_type=F32)

    @pl.when(pl.program_id(0) == 0)
    def _():
        if before is None:
            out[...] = total[:rels]
        else:
            out[...] = before[...] + total[:rels]

    @pl.when(pl.program_id(0) != 0)
    def _():
        out[...] += total[:rels]


def combine(gathered, rels, width, before=None):
    batch = min(gathered.shape[0], 32)
    whole = pl.BlockSpec((rels, width), lambda i: (0, 0))
    kernel = combine_kernel
    operands, in_specs = [gathered], [pl.BlockSpec((batch,) + gathered.shape[1:], lambda i: (i, 0, 0))]
    if before is None:
        kernel = lambda held, out: combine_kernel(held, None, out)
    else:
        operands.append(before)
        in_specs.append(whole)
    return pl.pallas_call(
        kernel,
        out_shape=jax.ShapeDtypeStruct((rels, width), F32),
        grid=(gathered.shape[0] // batch,),
        in_specs=in_specs,
        out_specs=whole,
        compiler_params=pltpu.CompilerParams(vmem_limit_bytes=VMEM_BYTES),
        cost_estimate=pl.CostEstimate(
            flops=4 * rels * gathered.shape[0] * 32 * width, bytes_accessed=2 << 20, transcendentals=0
        ),
        name="combine",
    )(*operands)


def spec(space):
    return pl.BlockSpec(memory_space=space)


def permute(value, shards, reps, shift, flip):
    route = [
        (s * reps + r, (s + shift) % shards * reps + (r ^ flip)) for s in range(shards) for r in range(reps)
    ]
    return lax.ppermute(value, AXES, route)


def exchange(held, bits, index, total):
    ways = 1 << len(bits)
    parts = [held]
    code = sum(((index >> bit) & 1) << i for i, bit in enumerate(bits))
    for k in range(1, ways):
        flip = sum(((k >> i) & 1) << bit for i, bit in enumerate(bits))
        parts.append(lax.ppermute(held, AXES, [(d, d ^ flip) for d in range(total)]))
    for i in range(len(bits)):
        swap = ((code >> i) & 1) == 1
        swapped = [parts[k ^ (1 << i)] for k in range(ways)]
        parts = [jnp.where(swap, b, a) for a, b in zip(parts, swapped)]
    return jnp.concatenate(parts, axis=0)


def local(shards, reps, entity, rel_weight, tile_rel, tile_head, tile_tail, tile_mask, negatives, tile_count):
    tiles = tile_rel.shape[0]
    block, width = entity.shape
    rels = rel_weight.shape[0]
    partition = block * reps
    smem, vmem = spec(pltpu.SMEM), spec(pltpu.VMEM)
    params = pltpu.CompilerParams(vmem_limit_bytes=VMEM_BYTES)

    others = [permute(entity, shards, reps, 0, k) for k in range(1, reps)]
    tails = [permute(entity, shards, reps, 1, k) for k in range(reps)]
    counts, weights, names, own = pl.pallas_call(
        prepare_kernel,
        out_shape=(
            jax.ShapeDtypeStruct((tiles, partition), F32),
            jax.ShapeDtypeStruct((tiles, width), F32),
            jax.ShapeDtypeStruct((1, LANES), F32),
            jax.ShapeDtypeStruct(entity.shape, F32),
        ),
        in_specs=[smem] + [spec(pl.ANY)] * 4,
        out_specs=(vmem, vmem, vmem, vmem),
        scratch_shapes=[
            pltpu.SMEM(tile_rel.shape, jnp.int32),
            pltpu.VMEM(negatives.shape, jnp.int32),
            pltpu.VMEM(rel_weight.shape, F32),
            pltpu.SemaphoreType.DMA((4,)),
        ],
        compiler_params=params,
        cost_estimate=pl.CostEstimate(flops=2 * tiles * partition * 256, bytes_accessed=4 << 20, transcendentals=0),
        name="prepare",
    )(tile_count, tile_rel, negatives, rel_weight, entity)
    mask = tile_mask.astype(F32)
    place = lax.axis_index("rep").astype(jnp.int32)[None]
    pieces = jax.ShapeDtypeStruct((reps, block, width), F32)
    terms, head_parts, tail_parts = pl.pallas_call(
        functools.partial(tiles_kernel, reps),
        out_shape=[jax.ShapeDtypeStruct((2 * tiles + SUBLANES, LANES), F32), pieces, pieces],
        in_specs=[smem] * 2 + [spec(pl.ANY)] * 2 + [vmem] * (2 * reps + 4),
        out_specs=[vmem] * 3,
        scratch_shapes=[pltpu.VMEM((reps, block, width), F32)] * 4
        + [pltpu.SMEM((tiles,), jnp.int32)] * 2
        + [pltpu.SemaphoreType.DMA((2,))],
        compiler_params=params,
        cost_estimate=pl.CostEstimate(
            flops=18 * tiles * block * partition * width, bytes_accessed=4 << 20, transcendentals=0
        ),
        name="tiles",
    )(tile_count, place, tile_head, tile_tail, own, *others, *tails, mask, counts, weights, names)

    total = shards * reps
    low = reps.bit_length() - 1
    top = total.bit_length() - 1
    order = list(range(top - 1, low, -1)) + list(range(low - 1, -1, -1))
    index = lax.axis_index("shard") * reps + lax.axis_index("rep")
    returned = permute(tail_parts, shards, reps, -1, 0)
    held = exchange(terms[None], order[:2], index, total)
    for i in range(2, len(order), 2):
        held = exchange(held, order[i : i + 2], index, total)
    held, returned = lax.optimization_barrier((held, returned))
    theirs = lax.ppermute(held, AXES, [(d, d ^ (1 << low)) for d in range(total)])
    arrived = [permute(head_parts[k] + returned[k], shards, reps, 0, k) for k in range(1, reps)]
    half = combine(held, rels, width)
    rel_grad = combine(theirs, rels, width, half)
    entity_grad, _ = lax.optimization_barrier((head_parts[0] + returned[0], rel_grad))
    for part in arrived:
        entity_grad = entity_grad + part
    return (entity_grad, rel_grad)


def solution(mesh):
    sizes = dict(mesh.shape)
    return jax.shard_map(
        functools.partial(local, sizes["shard"], sizes["rep"]),
        mesh=mesh,
        in_specs=(
            P(AXES, None),
            P(),
            P(AXES),
            P(AXES),
            P(AXES),
            P(AXES, None, None),
            P(AXES, None),
            P(AXES),
        ),
        out_specs=(P(AXES, None), P()),
        check_vma=False,
    )
```

```python
import functools

import jax
import jax.numpy as jnp
from jax import lax
from jax.experimental import pallas as pl
from jax.experimental.pallas import tpu as pltpu
from jax.sharding import PartitionSpec as P

AXES = ("shard", "rep")
F32 = jnp.float32
BF16 = jnp.bfloat16
GROUP = 2
AHEAD = 1
LANES = 128
SUBLANES = 8
VMEM_BYTES = 40 * 1024 * 1024
LOG2E = 1.4426950408889634


def halves(value):
    high = value.astype(BF16)
    low = (value - high.astype(F32)).astype(BF16)
    return high, low


def stacked_left(pair, axis):
    return jnp.concatenate([pair[0], pair[0], pair[1]], axis=axis)


def stacked_right(pair, axis):
    return jnp.concatenate([pair[0], pair[1], pair[0]], axis=axis)


def dot(left, right, left_axis, right_axis):
    return lax.dot_general(
        left,
        right,
        dimension_numbers=(((left_axis,), (right_axis,)), ((), ())),
        preferred_element_type=F32,
    )


def prepare_kernel(count, rel_ids, negatives, rel_weight, entity, *refs):
    counts_out, weights_out, names_out, entity_out = refs[:4]
    ids, draws, table, sems = refs[4:]
    tiles, partition = counts_out.shape
    copies = [
        pltpu.make_async_copy(source, target, sems.at[i])
        for i, (source, target) in enumerate(
            [(rel_ids, ids), (negatives, draws), (rel_weight, table), (entity, entity_out)]
        )
    ]
    for copy in copies:
        copy.start()
    copies[1].wait()
    chosen = draws[...]
    columns = lax.broadcasted_iota(jnp.int32, (tiles, partition), 1)
    total = jnp.zeros((tiles, partition), F32)
    for draw in range(chosen.shape[1]):
        total = total + jnp.where(chosen[:, draw : draw + 1] == columns, 1.0, 0.0)
    slots = lax.broadcasted_iota(jnp.int32, (tiles, partition), 0)
    counts_out[...] = jnp.where(slots < count[0], total, 0.0)
    copies[0].wait()
    copies[2].wait()
    lanes = lax.broadcasted_iota(jnp.int32, (1, LANES), 1) % tiles
    names = jnp.zeros((1, LANES), jnp.int32)
    for tile in range(tiles):
        weights_out[tile : tile + 1, :] = table[pl.ds(ids[tile], 1), :]
        names = jnp.where(lanes == tile, ids[tile], names)
    names_out[...] = names.astype(F32)
    copies[3].wait()


def tiles_kernel(blocks, *refs):
    count, place, head_in_ids, tail_in_ids = refs[:4]
    head_in = refs[4 : 4 + blocks]
    tail_in = refs[4 + blocks : 4 + 2 * blocks]
    mask, counts, weights, names = refs[4 + 2 * blocks : 8 + 2 * blocks]
    terms = refs[8 + 2 * blocks]
    head_out, tail_out = refs[9 + 2 * blocks : 11 + 2 * blocks]
    heads, tails, head_grad, tail_grad, head_ids, tail_ids, sems = refs[11 + 2 * blocks :]
    tiles, block, _ = mask.shape
    width = weights.shape[1]
    mine = place[0]
    copies = [
        pltpu.make_async_copy(head_in_ids, head_ids, sems.at[0]),
        pltpu.make_async_copy(tail_in_ids, tail_ids, sems.at[1]),
    ]
    for copy in copies:
        copy.start()
    for k in range(blocks):
        heads[mine ^ k] = head_in[k][...]
        tails[mine ^ k] = tail_in[k][...]
    head_grad[...] = jnp.zeros_like(head_grad)
    terms[2 * tiles :, :] = jnp.zeros((terms.shape[0] - 2 * tiles, LANES), F32)
    terms[2 * tiles : 2 * tiles + 1, :] = names[...]
    tail = tails[...].reshape(blocks * block, width)
    for_scores = stacked_right(halves(tail * -LOG2E), 1)
    for_mixed = stacked_right(halves(tail), 0)
    for copy in copies:
        copy.wait()

    def start(base):
        rows = [heads[head_ids[slot]] for slot in range(base, base + GROUP)]
        scales = [weights[slot : slot + 1, :] for slot in range(base, base + GROUP)]
        scaled = halves(jnp.concatenate([a * b for a, b in zip(rows, scales)], axis=0))
        return rows, scales, scaled, dot(stacked_left(scaled, 1), for_scores, 1, 1)

    def weigh(base, scores):
        grads = []
        for u, slot in enumerate(range(base, base + GROUP)):
            adjacent = mask[slot]
            live = slot < count[0]
            parts = []
            for b in range(blocks):
                flag = jnp.where(jnp.logical_and(live, tail_ids[slot] == b), 1.0, 0.0)
                times = counts[slot : slot + 1, b * block : (b + 1) * block]
                score = scores[u * block : (u + 1) * block, b * block : (b + 1) * block]
                odds = jnp.exp2(jnp.minimum(score, 115.0))
                parts.append((times - (adjacent * flag) * odds) / (1.0 + odds))
            grads.append(jnp.concatenate(parts, axis=1))
        return halves(jnp.concatenate(grads, axis=0))

    ahead = [start(base) for base in range(0, AHEAD * GROUP, GROUP)]
    for base in range(0, tiles, GROUP):
        if base + AHEAD * GROUP < tiles:
            ahead.append(start(base + AHEAD * GROUP))
        rows, scales, scaled, scores = ahead.pop(0)
        grads = weigh(base, scores)
        mixed = dot(stacked_left(grads, 1), for_mixed, 1, 0)
        for u, slot in enumerate(range(base, base + GROUP)):
            part = mixed[u * block : (u + 1) * block, :]
            term = jnp.sum(rows[u] * part, axis=0, keepdims=True)
            terms[slot : slot + 1, :] = term[:, :LANES]
            terms[tiles + slot : tiles + slot + 1, :] = term[:, LANES:]
            head_grad[head_ids[slot]] += part * scales[u]
        tail_part = dot(stacked_left(grads, 0), stacked_right(scaled, 0), 0, 0).reshape(tail_grad.shape)
        if base == 0:
            tail_grad[...] = tail_part
        else:
            tail_grad[...] += tail_part

    for k in range(blocks):
        head_out[k] = head_grad[mine ^ k]
        tail_out[k] = tail_grad[mine ^ k]


def combine_kernel(gathered, before, out):
    devices = gathered.shape[0]
    tiles = (gathered.shape[1] - SUBLANES) // 2
    rels, width = out.shape
    padded = -(-rels // SUBLANES) * SUBLANES
    share = LANES // tiles
    lanes = lax.broadcasted_iota(jnp.int32, (1, LANES), 1) // tiles
    rows = lax.broadcasted_iota(jnp.int32, (padded, LANES), 0)
    hits = []
    for first in range(0, devices, share):
        names = gathered[first, 2 * tiles : 2 * tiles + 1, :]
        for other in range(1, share):
            names = jnp.where(lanes == other, gathered[first + other, 2 * tiles : 2 * tiles + 1, :], names)
        hits.append(jnp.where(rows == names.astype(jnp.int32), 1.0, 0.0).astype(BF16))
    hits = jnp.concatenate(hits, axis=1)
    left = gathered[:, :tiles, :].reshape(devices * tiles, LANES)
    right = gathered[:, tiles : 2 * tiles, :].reshape(devices * tiles, LANES)
    high, low = halves(jnp.concatenate([left, right], axis=1))
    total = jnp.dot(hits, high, preferred_element_type=F32) + jnp.dot(hits, low, preferred_element_type=F32)

    @pl.when(pl.program_id(0) == 0)
    def _():
        if before is None:
            out[...] = total[:rels]
        else:
            out[...] = before[...] + total[:rels]

    @pl.when(pl.program_id(0) != 0)
    def _():
        out[...] += total[:rels]


def combine(gathered, rels, width, before=None):
    batch = min(gathered.shape[0], 32)
    whole = pl.BlockSpec((rels, width), lambda i: (0, 0))
    kernel = combine_kernel
    operands, in_specs = [gathered], [pl.BlockSpec((batch,) + gathered.shape[1:], lambda i: (i, 0, 0))]
    if before is None:
        kernel = lambda held, out: combine_kernel(held, None, out)
    else:
        operands.append(before)
        in_specs.append(whole)
    return pl.pallas_call(
        kernel,
        out_shape=jax.ShapeDtypeStruct((rels, width), F32),
        grid=(gathered.shape[0] // batch,),
        in_specs=in_specs,
        out_specs=whole,
        compiler_params=pltpu.CompilerParams(vmem_limit_bytes=VMEM_BYTES),
        cost_estimate=pl.CostEstimate(
            flops=4 * rels * gathered.shape[0] * 32 * width, bytes_accessed=2 << 20, transcendentals=0
        ),
        name="combine",
    )(*operands)


def spec(space):
    return pl.BlockSpec(memory_space=space)


def permute(value, shards, reps, shift, flip):
    route = [
        (s * reps + r, (s + shift) % shards * reps + (r ^ flip)) for s in range(shards) for r in range(reps)
    ]
    return lax.ppermute(value, AXES, route)


def exchange(held, bits, index, total):
    ways = 1 << len(bits)
    parts = [held]
    code = sum(((index >> bit) & 1) << i for i, bit in enumerate(bits))
    for k in range(1, ways):
        flip = sum(((k >> i) & 1) << bit for i, bit in enumerate(bits))
        parts.append(lax.ppermute(held, AXES, [(d, d ^ flip) for d in range(total)]))
    for i in range(len(bits)):
        swap = ((code >> i) & 1) == 1
        swapped = [parts[k ^ (1 << i)] for k in range(ways)]
        parts = [jnp.where(swap, b, a) for a, b in zip(parts, swapped)]
    return jnp.concatenate(parts, axis=0)


def local(shards, reps, entity, rel_weight, tile_rel, tile_head, tile_tail, tile_mask, negatives, tile_count):
    tiles = tile_rel.shape[0]
    block, width = entity.shape
    rels = rel_weight.shape[0]
    partition = block * reps
    smem, vmem = spec(pltpu.SMEM), spec(pltpu.VMEM)
    params = pltpu.CompilerParams(vmem_limit_bytes=VMEM_BYTES)

    others = [permute(entity, shards, reps, 0, k) for k in range(1, reps)]
    tails = [permute(entity, shards, reps, 1, k) for k in range(reps)]
    counts, weights, names, own = pl.pallas_call(
        prepare_kernel,
        out_shape=(
            jax.ShapeDtypeStruct((tiles, partition), F32),
            jax.ShapeDtypeStruct((tiles, width), F32),
            jax.ShapeDtypeStruct((1, LANES), F32),
            jax.ShapeDtypeStruct(entity.shape, F32),
        ),
        in_specs=[smem] + [spec(pl.ANY)] * 4,
        out_specs=(vmem, vmem, vmem, vmem),
        scratch_shapes=[
            pltpu.SMEM(tile_rel.shape, jnp.int32),
            pltpu.VMEM(negatives.shape, jnp.int32),
            pltpu.VMEM(rel_weight.shape, F32),
            pltpu.SemaphoreType.DMA((4,)),
        ],
        compiler_params=params,
        cost_estimate=pl.CostEstimate(flops=2 * tiles * partition * 256, bytes_accessed=4 << 20, transcendentals=0),
        name="prepare",
    )(tile_count, tile_rel, negatives, rel_weight, entity)
    mask = tile_mask.astype(F32)
    place = lax.axis_index("rep").astype(jnp.int32)[None]
    pieces = jax.ShapeDtypeStruct((reps, block, width), F32)
    terms, head_parts, tail_parts = pl.pallas_call(
        functools.partial(tiles_kernel, reps),
        out_shape=[jax.ShapeDtypeStruct((2 * tiles + SUBLANES, LANES), F32), pieces, pieces],
        in_specs=[smem] * 2 + [spec(pl.ANY)] * 2 + [vmem] * (2 * reps + 4),
        out_specs=[vmem] * 3,
        scratch_shapes=[pltpu.VMEM((reps, block, width), F32)] * 4
        + [pltpu.SMEM((tiles,), jnp.int32)] * 2
        + [pltpu.SemaphoreType.DMA((2,))],
        compiler_params=params,
        cost_estimate=pl.CostEstimate(
            flops=18 * tiles * block * partition * width, bytes_accessed=4 << 20, transcendentals=0
        ),
        name="tiles",
    )(tile_count, place, tile_head, tile_tail, own, *others, *tails, mask, counts, weights, names)

    total = shards * reps
    low = reps.bit_length() - 1
    top = total.bit_length() - 1
    order = list(range(top - 1, low, -1)) + list(range(low - 1, -1, -1))
    index = lax.axis_index("shard") * reps + lax.axis_index("rep")
    returned = permute(tail_parts, shards, reps, -1, 0)
    held = exchange(terms[None], order[:2], index, total)
    for i in range(2, len(order), 2):
        held = exchange(held, order[i : i + 2], index, total)
    held, returned = lax.optimization_barrier((held, returned))
    theirs = lax.ppermute(held, AXES, [(d, d ^ (1 << low)) for d in range(total)])
    arrived = [permute(head_parts[k] + returned[k], shards, reps, 0, k) for k in range(1, reps)]
    half = combine(held, rels, width)
    rel_grad = combine(theirs, rels, width, half)
    entity_grad, _ = lax.optimization_barrier((head_parts[0] + returned[0], rel_grad))
    for part in arrived:
        entity_grad = entity_grad + part
    return (entity_grad, rel_grad)


def solution(mesh):
    sizes = dict(mesh.shape)
    return jax.shard_map(
        functools.partial(local, sizes["shard"], sizes["rep"]),
        mesh=mesh,
        in_specs=(
            P(AXES, None),
            P(),
            P(AXES),
            P(AXES),
            P(AXES),
            P(AXES, None, None),
            P(AXES, None),
            P(AXES),
        ),
        out_specs=(P(AXES, None), P()),
        check_vma=False,
    )
```

```python
import functools

import jax
import jax.numpy as jnp
from jax import lax
from jax.experimental import pallas as pl
from jax.experimental.pallas import tpu as pltpu
from jax.sharding import PartitionSpec as P

AXES = ("shard", "rep")
F32 = jnp.float32
BF16 = jnp.bfloat16
GROUP = 2
AHEAD = 1
LANES = 128
SUBLANES = 8
MIB = 1024 * 1024
LOG2E = 1.4426950408889634


def halves(value):
    high = value.astype(BF16)
    low = (value - high.astype(F32)).astype(BF16)
    return high, low


def stacked_left(pair, axis):
    return jnp.concatenate([pair[0], pair[0], pair[1]], axis=axis)


def stacked_right(pair, axis):
    return jnp.concatenate([pair[0], pair[1], pair[0]], axis=axis)


def dot(left, right, left_axis, right_axis):
    return lax.dot_general(
        left,
        right,
        dimension_numbers=(((left_axis,), (right_axis,)), ((), ())),
        preferred_element_type=F32,
    )


def prepare_kernel(count, rel_ids, negatives, rel_weight, entity, *refs):
    counts_out, weights_out, names_out, entity_out = refs[:4]
    ids, draws, table, sems = refs[4:]
    tiles, partition = counts_out.shape
    copies = [
        pltpu.make_async_copy(source, target, sems.at[i])
        for i, (source, target) in enumerate(
            [(rel_ids, ids), (negatives, draws), (rel_weight, table), (entity, entity_out)]
        )
    ]
    for copy in copies:
        copy.start()
    copies[1].wait()
    chosen = draws[...]
    columns = lax.broadcasted_iota(jnp.int32, (tiles, partition), 1)
    total = jnp.zeros((tiles, partition), F32)
    for draw in range(chosen.shape[1]):
        total = total + jnp.where(chosen[:, draw : draw + 1] == columns, 1.0, 0.0)
    slots = lax.broadcasted_iota(jnp.int32, (tiles, partition), 0)
    counts_out[...] = jnp.where(slots < count[0], total, 0.0)
    copies[0].wait()
    copies[2].wait()
    lanes = lax.broadcasted_iota(jnp.int32, (1, LANES), 1) % tiles
    names = jnp.zeros((1, LANES), jnp.int32)
    for tile in range(tiles):
        weights_out[tile : tile + 1, :] = table[pl.ds(ids[tile], 1), :]
        names = jnp.where(lanes == tile, ids[tile], names)
    names_out[...] = names.astype(F32)
    copies[3].wait()


def tiles_kernel(blocks, *refs):
    count, place, head_in_ids, tail_in_ids = refs[:4]
    head_in = refs[4 : 4 + blocks]
    tail_in = refs[4 + blocks : 4 + 2 * blocks]
    mask, counts, weights, names = refs[4 + 2 * blocks : 8 + 2 * blocks]
    terms = refs[8 + 2 * blocks]
    head_out, heads, grads_high, grads_low = refs[9 + 2 * blocks : 13 + 2 * blocks]
    tails, head_grad, head_ids, tail_ids, sems = refs[13 + 2 * blocks :]
    tiles, block, _ = mask.shape
    width = weights.shape[1]
    mine = place[0]
    copies = [
        pltpu.make_async_copy(head_in_ids, head_ids, sems.at[0]),
        pltpu.make_async_copy(tail_in_ids, tail_ids, sems.at[1]),
    ]
    for copy in copies:
        copy.start()
    for k in range(blocks):
        heads[mine ^ k] = head_in[k][...]
        tails[mine ^ k] = tail_in[k][...]
    head_grad[...] = jnp.zeros_like(head_grad)
    terms[2 * tiles :, :] = jnp.zeros((terms.shape[0] - 2 * tiles, LANES), F32)
    terms[2 * tiles : 2 * tiles + 1, :] = names[...]
    tail = tails[...].reshape(blocks * block, width)
    for_scores = stacked_right(halves(tail * -LOG2E), 1)
    for_mixed = stacked_right(halves(tail), 0)
    for copy in copies:
        copy.wait()

    def start(base):
        rows = [heads[head_ids[slot]] for slot in range(base, base + GROUP)]
        scales = [weights[slot : slot + 1, :] for slot in range(base, base + GROUP)]
        scaled = halves(jnp.concatenate([a * b for a, b in zip(rows, scales)], axis=0))
        return rows, scales, scaled, dot(stacked_left(scaled, 1), for_scores, 1, 1)

    def weigh(base, scores):
        grads = []
        for u, slot in enumerate(range(base, base + GROUP)):
            adjacent = mask[slot]
            live = slot < count[0]
            parts = []
            for b in range(blocks):
                flag = jnp.where(jnp.logical_and(live, tail_ids[slot] == b), 1.0, 0.0)
                times = counts[slot : slot + 1, b * block : (b + 1) * block]
                score = scores[u * block : (u + 1) * block, b * block : (b + 1) * block]
                odds = jnp.exp2(jnp.minimum(score, 115.0))
                parts.append((times - (adjacent * flag) * odds) / (1.0 + odds))
            grads.append(jnp.concatenate(parts, axis=1))
        return halves(jnp.concatenate(grads, axis=0))

    ahead = [start(base) for base in range(0, AHEAD * GROUP, GROUP)]
    for base in range(0, tiles, GROUP):
        if base + AHEAD * GROUP < tiles:
            ahead.append(start(base + AHEAD * GROUP))
        rows, scales, scaled, scores = ahead.pop(0)
        grads = weigh(base, scores)
        mixed = dot(stacked_left(grads, 1), for_mixed, 1, 0)
        for u, slot in enumerate(range(base, base + GROUP)):
            part = mixed[u * block : (u + 1) * block, :]
            term = jnp.sum(rows[u] * part, axis=0, keepdims=True)
            terms[slot : slot + 1, :] = term[:, :LANES]
            terms[tiles + slot : tiles + slot + 1, :] = term[:, LANES:]
            head_grad[head_ids[slot]] += part * scales[u]
        here = slice(base * block, (base + GROUP) * block)
        grads_high[here, :] = grads[0]
        grads_low[here, :] = grads[1]

    for k in range(blocks):
        head_out[k] = head_grad[mine ^ k]


def tails_kernel(place, head_in_ids, heads, weights, grads_high, grads_low, tail_out, tail_grad, head_ids, sem):
    blocks, block, _ = heads.shape
    tiles = weights.shape[0]
    copy = pltpu.make_async_copy(head_in_ids, head_ids, sem)
    copy.start()
    copy.wait()
    for base in range(0, tiles, GROUP):
        here = slice(base * block, (base + GROUP) * block)
        scaled = [heads[head_ids[slot]] * weights[slot : slot + 1, :] for slot in range(base, base + GROUP)]
        scaled = halves(jnp.concatenate(scaled, axis=0))
        grads = grads_high[here, :], grads_low[here, :]
        part = dot(stacked_left(grads, 0), stacked_right(scaled, 0), 0, 0).reshape(tail_grad.shape)
        if base == 0:
            tail_grad[...] = part
        else:
            tail_grad[...] += part
    for k in range(blocks):
        tail_out[k] = tail_grad[place[0] ^ k]


def combine_kernel(gathered, before, out):
    devices = gathered.shape[0]
    tiles = (gathered.shape[1] - SUBLANES) // 2
    rels, width = out.shape
    padded = -(-rels // SUBLANES) * SUBLANES
    share = LANES // tiles
    lanes = lax.broadcasted_iota(jnp.int32, (1, LANES), 1) // tiles
    rows = lax.broadcasted_iota(jnp.int32, (padded, LANES), 0)
    hits = []
    for first in range(0, devices, share):
        names = gathered[first, 2 * tiles : 2 * tiles + 1, :]
        for other in range(1, share):
            names = jnp.where(lanes == other, gathered[first + other, 2 * tiles : 2 * tiles + 1, :], names)
        hits.append(jnp.where(rows == names.astype(jnp.int32), 1.0, 0.0).astype(BF16))
    hits = jnp.concatenate(hits, axis=1)
    left = gathered[:, :tiles, :].reshape(devices * tiles, LANES)
    right = gathered[:, tiles : 2 * tiles, :].reshape(devices * tiles, LANES)
    high, low = halves(jnp.concatenate([left, right], axis=1))
    total = jnp.dot(hits, high, preferred_element_type=F32) + jnp.dot(hits, low, preferred_element_type=F32)

    @pl.when(pl.program_id(0) == 0)
    def _():
        if before is None:
            out[...] = total[:rels]
        else:
            out[...] = before[...] + total[:rels]

    @pl.when(pl.program_id(0) != 0)
    def _():
        out[...] += total[:rels]


def combine(gathered, rels, width, before=None):
    batch = min(gathered.shape[0], 32)
    whole = pl.BlockSpec((rels, width), lambda i: (0, 0))
    kernel = combine_kernel
    operands, in_specs = [gathered], [pl.BlockSpec((batch,) + gathered.shape[1:], lambda i: (i, 0, 0))]
    if before is None:
        kernel = lambda held, out: combine_kernel(held, None, out)
    else:
        operands.append(before)
        in_specs.append(whole)
    return pl.pallas_call(
        kernel,
        out_shape=jax.ShapeDtypeStruct((rels, width), F32),
        grid=(gathered.shape[0] // batch,),
        in_specs=in_specs,
        out_specs=whole,
        compiler_params=pltpu.CompilerParams(vmem_limit_bytes=24 * MIB),
        cost_estimate=pl.CostEstimate(
            flops=4 * rels * gathered.shape[0] * 32 * width, bytes_accessed=2 << 20, transcendentals=0
        ),
        name="combine",
    )(*operands)


def spec(space):
    return pl.BlockSpec(memory_space=space)


def permute(value, shards, reps, shift, flip):
    route = [
        (s * reps + r, (s + shift) % shards * reps + (r ^ flip)) for s in range(shards) for r in range(reps)
    ]
    return lax.ppermute(value, AXES, route)


def exchange(held, bits, index, total):
    ways = 1 << len(bits)
    parts = [held]
    code = sum(((index >> bit) & 1) << i for i, bit in enumerate(bits))
    for k in range(1, ways):
        flip = sum(((k >> i) & 1) << bit for i, bit in enumerate(bits))
        parts.append(lax.ppermute(held, AXES, [(d, d ^ flip) for d in range(total)]))
    for i in range(len(bits)):
        swap = ((code >> i) & 1) == 1
        swapped = [parts[k ^ (1 << i)] for k in range(ways)]
        parts = [jnp.where(swap, b, a) for a, b in zip(parts, swapped)]
    return jnp.concatenate(parts, axis=0)


def local(shards, reps, entity, rel_weight, tile_rel, tile_head, tile_tail, tile_mask, negatives, tile_count):
    tiles = tile_rel.shape[0]
    block, width = entity.shape
    rels = rel_weight.shape[0]
    partition = block * reps
    smem, vmem = spec(pltpu.SMEM), spec(pltpu.VMEM)
    params = pltpu.CompilerParams(vmem_limit_bytes=min(8 * reps, 48) * MIB)

    others = [permute(entity, shards, reps, 0, k) for k in range(1, reps)]
    tails = [permute(entity, shards, reps, 1, k) for k in range(reps)]
    counts, weights, names, own = pl.pallas_call(
        prepare_kernel,
        out_shape=(
            jax.ShapeDtypeStruct((tiles, partition), F32),
            jax.ShapeDtypeStruct((tiles, width), F32),
            jax.ShapeDtypeStruct((1, LANES), F32),
            jax.ShapeDtypeStruct(entity.shape, F32),
        ),
        in_specs=[smem] + [spec(pl.ANY)] * 4,
        out_specs=(vmem, vmem, vmem, vmem),
        scratch_shapes=[
            pltpu.SMEM(tile_rel.shape, jnp.int32),
            pltpu.VMEM(negatives.shape, jnp.int32),
            pltpu.VMEM(rel_weight.shape, F32),
            pltpu.SemaphoreType.DMA((4,)),
        ],
        compiler_params=params,
        cost_estimate=pl.CostEstimate(flops=2 * tiles * partition * 256, bytes_accessed=4 << 20, transcendentals=0),
        name="prepare",
    )(tile_count, tile_rel, negatives, rel_weight, entity)
    mask = tile_mask.astype(F32)
    place = lax.axis_index("rep").astype(jnp.int32)[None]
    pieces = jax.ShapeDtypeStruct((reps, block, width), F32)
    coefficients = jax.ShapeDtypeStruct((tiles * block, partition), BF16)
    terms, head_parts, heads, grads_high, grads_low = pl.pallas_call(
        functools.partial(tiles_kernel, reps),
        out_shape=[jax.ShapeDtypeStruct((2 * tiles + SUBLANES, LANES), F32), pieces, pieces]
        + [coefficients] * 2,
        in_specs=[smem] * 2 + [spec(pl.ANY)] * 2 + [vmem] * (2 * reps + 4),
        out_specs=[vmem] * 5,
        scratch_shapes=[pltpu.VMEM((reps, block, width), F32)] * 2
        + [pltpu.SMEM((tiles,), jnp.int32)] * 2
        + [pltpu.SemaphoreType.DMA((2,))],
        compiler_params=params,
        cost_estimate=pl.CostEstimate(
            flops=12 * tiles * block * partition * width, bytes_accessed=4 << 20, transcendentals=0
        ),
        name="tiles",
    )(tile_count, place, tile_head, tile_tail, own, *others, *tails, mask, counts, weights, names)
    tail_parts = pl.pallas_call(
        tails_kernel,
        out_shape=pieces,
        in_specs=[smem, spec(pl.ANY)] + [vmem] * 4,
        out_specs=vmem,
        scratch_shapes=[
            pltpu.VMEM((reps, block, width), F32),
            pltpu.SMEM((tiles,), jnp.int32),
            pltpu.SemaphoreType.DMA,
        ],
        compiler_params=params,
        cost_estimate=pl.CostEstimate(
            flops=6 * tiles * block * partition * width, bytes_accessed=4 << 20, transcendentals=0
        ),
        name="tails",
    )(place, tile_head, heads, weights, grads_high, grads_low)

    total = shards * reps
    low = reps.bit_length() - 1
    top = total.bit_length() - 1
    order = list(range(top - 1, low, -1)) + list(range(low - 1, -1, -1))
    index = lax.axis_index("shard") * reps + lax.axis_index("rep")
    held = exchange(terms[None], order[:2], index, total)
    held, tail_parts = lax.optimization_barrier((held, tail_parts))
    returned = permute(tail_parts, shards, reps, -1, 0)
    for i in range(2, len(order), 2):
        held = exchange(held, order[i : i + 2], index, total)
    held, returned = lax.optimization_barrier((held, returned))
    theirs = lax.ppermute(held, AXES, [(d, d ^ (1 << low)) for d in range(total)])
    arrived = [permute(head_parts[k] + returned[k], shards, reps, 0, k) for k in range(1, reps)]
    half = combine(held, rels, width)
    rel_grad = combine(theirs, rels, width, half)
    entity_grad, _ = lax.optimization_barrier((head_parts[0] + returned[0], rel_grad))
    for part in arrived:
        entity_grad = entity_grad + part
    return (entity_grad, rel_grad)


def solution(mesh):
    sizes = dict(mesh.shape)
    return jax.shard_map(
        functools.partial(local, sizes["shard"], sizes["rep"]),
        mesh=mesh,
        in_specs=(
            P(AXES, None),
            P(),
            P(AXES),
            P(AXES),
            P(AXES),
            P(AXES, None, None),
            P(AXES, None),
            P(AXES),
        ),
        out_specs=(P(AXES, None), P()),
        check_vma=False,
    )
```

```python
import functools

import jax
import jax.numpy as jnp
from jax import lax
from jax.experimental import pallas as pl
from jax.experimental.pallas import tpu as pltpu
from jax.sharding import PartitionSpec as P

AXES = ("shard", "rep")
F32 = jnp.float32
BF16 = jnp.bfloat16
GROUP = 2
AHEAD = 1
LANES = 128
SUBLANES = 8
MIB = 1024 * 1024
LOG2E = 1.4426950408889634


def halves(value):
    high = value.astype(BF16)
    low = (value - high.astype(F32)).astype(BF16)
    return high, low


def stacked_left(pair, axis):
    return jnp.concatenate([pair[0], pair[0], pair[1]], axis=axis)


def stacked_right(pair, axis):
    return jnp.concatenate([pair[0], pair[1], pair[0]], axis=axis)


def dot(left, right, left_axis, right_axis):
    return lax.dot_general(
        left,
        right,
        dimension_numbers=(((left_axis,), (right_axis,)), ((), ())),
        preferred_element_type=F32,
    )


def prepare_kernel(count, rel_ids, negatives, rel_weight, entity, *refs):
    counts_out, weights_out, names_out, entity_out = refs[:4]
    ids, draws, table, sems = refs[4:]
    tiles, partition = counts_out.shape
    copies = [
        pltpu.make_async_copy(source, target, sems.at[i])
        for i, (source, target) in enumerate(
            [(rel_ids, ids), (negatives, draws), (rel_weight, table), (entity, entity_out)]
        )
    ]
    for copy in copies:
        copy.start()
    copies[1].wait()
    chosen = draws[...]
    columns = lax.broadcasted_iota(jnp.int32, (tiles, partition), 1)
    total = jnp.zeros((tiles, partition), F32)
    for draw in range(chosen.shape[1]):
        total = total + jnp.where(chosen[:, draw : draw + 1] == columns, 1.0, 0.0)
    slots = lax.broadcasted_iota(jnp.int32, (tiles, partition), 0)
    counts_out[...] = jnp.where(slots < count[0], total, 0.0)
    copies[0].wait()
    copies[2].wait()
    lanes = lax.broadcasted_iota(jnp.int32, (1, LANES), 1) % tiles
    names = jnp.zeros((1, LANES), jnp.int32)
    for tile in range(tiles):
        weights_out[tile : tile + 1, :] = table[pl.ds(ids[tile], 1), :]
        names = jnp.where(lanes == tile, ids[tile], names)
    names_out[...] = names.astype(F32)
    copies[3].wait()


def tiles_kernel(blocks, *refs):
    count, place, head_in_ids, tail_in_ids = refs[:4]
    tail_in = refs[4 : 4 + blocks][::-1]
    head_in = refs[4 + blocks : 4 + 2 * blocks]
    mask, counts, weights, names = refs[4 + 2 * blocks : 8 + 2 * blocks]
    terms = refs[8 + 2 * blocks]
    head_out, heads, grads_high, grads_low = refs[9 + 2 * blocks : 13 + 2 * blocks]
    tails, head_grad, head_ids, tail_ids, sems = refs[13 + 2 * blocks :]
    tiles, block, _ = mask.shape
    width = weights.shape[1]
    mine = place[0]
    copies = [
        pltpu.make_async_copy(head_in_ids, head_ids, sems.at[0]),
        pltpu.make_async_copy(tail_in_ids, tail_ids, sems.at[1]),
    ]
    for copy in copies:
        copy.start()
    for k in range(blocks):
        heads[mine ^ k] = head_in[k][...]
        tails[mine ^ k] = tail_in[k][...]
    head_grad[...] = jnp.zeros_like(head_grad)
    terms[2 * tiles :, :] = jnp.zeros((terms.shape[0] - 2 * tiles, LANES), F32)
    terms[2 * tiles : 2 * tiles + 1, :] = names[...]
    tail = tails[...].reshape(blocks * block, width)
    for_scores = stacked_right(halves(tail * -LOG2E), 1)
    for_mixed = stacked_right(halves(tail), 0)
    for copy in copies:
        copy.wait()

    def start(base):
        rows = [heads[head_ids[slot]] for slot in range(base, base + GROUP)]
        scales = [weights[slot : slot + 1, :] for slot in range(base, base + GROUP)]
        scaled = halves(jnp.concatenate([a * b for a, b in zip(rows, scales)], axis=0))
        return rows, scales, scaled, dot(stacked_left(scaled, 1), for_scores, 1, 1)

    def weigh(base, scores):
        grads = []
        for u, slot in enumerate(range(base, base + GROUP)):
            adjacent = mask[slot]
            live = slot < count[0]
            parts = []
            for b in range(blocks):
                flag = jnp.where(jnp.logical_and(live, tail_ids[slot] == b), 1.0, 0.0)
                times = counts[slot : slot + 1, b * block : (b + 1) * block]
                score = scores[u * block : (u + 1) * block, b * block : (b + 1) * block]
                odds = jnp.exp2(jnp.minimum(score, 115.0))
                parts.append((times - (adjacent * flag) * odds) / (1.0 + odds))
            grads.append(jnp.concatenate(parts, axis=1))
        return halves(jnp.concatenate(grads, axis=0))

    ahead = [start(base) for base in range(0, AHEAD * GROUP, GROUP)]
    for base in range(0, tiles, GROUP):
        if base + AHEAD * GROUP < tiles:
            ahead.append(start(base + AHEAD * GROUP))
        rows, scales, scaled, scores = ahead.pop(0)
        grads = weigh(base, scores)
        mixed = dot(stacked_left(grads, 1), for_mixed, 1, 0)
        for u, slot in enumerate(range(base, base + GROUP)):
            part = mixed[u * block : (u + 1) * block, :]
            term = jnp.sum(rows[u] * part, axis=0, keepdims=True)
            terms[slot : slot + 1, :] = term[:, :LANES]
            terms[tiles + slot : tiles + slot + 1, :] = term[:, LANES:]
            head_grad[head_ids[slot]] += part * scales[u]
        here = slice(base * block, (base + GROUP) * block)
        grads_high[here, :] = grads[0]
        grads_low[here, :] = grads[1]

    for k in range(blocks):
        head_out[k] = head_grad[mine ^ k]


def tails_kernel(place, head_in_ids, heads, weights, grads_high, grads_low, tail_out, tail_grad, head_ids, sem):
    blocks, block, _ = heads.shape
    tiles = weights.shape[0]
    copy = pltpu.make_async_copy(head_in_ids, head_ids, sem)
    copy.start()
    copy.wait()
    for base in range(0, tiles, GROUP):
        here = slice(base * block, (base + GROUP) * block)
        scaled = [heads[head_ids[slot]] * weights[slot : slot + 1, :] for slot in range(base, base + GROUP)]
        scaled = halves(jnp.concatenate(scaled, axis=0))
        grads = grads_high[here, :], grads_low[here, :]
        part = dot(stacked_left(grads, 0), stacked_right(scaled, 0), 0, 0).reshape(tail_grad.shape)
        if base == 0:
            tail_grad[...] = part
        else:
            tail_grad[...] += part
    for k in range(blocks):
        tail_out[k] = tail_grad[place[0] ^ k]


def combine_kernel(gathered, before, out):
    devices = gathered.shape[0]
    tiles = (gathered.shape[1] - SUBLANES) // 2
    rels, width = out.shape
    padded = -(-rels // SUBLANES) * SUBLANES
    share = LANES // tiles
    lanes = lax.broadcasted_iota(jnp.int32, (1, LANES), 1) // tiles
    rows = lax.broadcasted_iota(jnp.int32, (padded, LANES), 0)
    hits = []
    for first in range(0, devices, share):
        names = gathered[first, 2 * tiles : 2 * tiles + 1, :]
        for other in range(1, share):
            names = jnp.where(lanes == other, gathered[first + other, 2 * tiles : 2 * tiles + 1, :], names)
        hits.append(jnp.where(rows == names.astype(jnp.int32), 1.0, 0.0).astype(BF16))
    hits = jnp.concatenate(hits, axis=1)
    left = gathered[:, :tiles, :].reshape(devices * tiles, LANES)
    right = gathered[:, tiles : 2 * tiles, :].reshape(devices * tiles, LANES)
    high, low = halves(jnp.concatenate([left, right], axis=1))
    total = jnp.dot(hits, high, preferred_element_type=F32) + jnp.dot(hits, low, preferred_element_type=F32)

    @pl.when(pl.program_id(0) == 0)
    def _():
        if before is None:
            out[...] = total[:rels]
        else:
            out[...] = before[...] + total[:rels]

    @pl.when(pl.program_id(0) != 0)
    def _():
        out[...] += total[:rels]


def combine(gathered, rels, width, before=None):
    batch = min(gathered.shape[0], 32)
    whole = pl.BlockSpec((rels, width), lambda i: (0, 0))
    kernel = combine_kernel
    operands, in_specs = [gathered], [pl.BlockSpec((batch,) + gathered.shape[1:], lambda i: (i, 0, 0))]
    if before is None:
        kernel = lambda held, out: combine_kernel(held, None, out)
    else:
        operands.append(before)
        in_specs.append(whole)
    return pl.pallas_call(
        kernel,
        out_shape=jax.ShapeDtypeStruct((rels, width), F32),
        grid=(gathered.shape[0] // batch,),
        in_specs=in_specs,
        out_specs=whole,
        compiler_params=pltpu.CompilerParams(vmem_limit_bytes=24 * MIB),
        cost_estimate=pl.CostEstimate(
            flops=4 * rels * gathered.shape[0] * 32 * width, bytes_accessed=2 << 20, transcendentals=0
        ),
        name="combine",
    )(*operands)


def spec(space):
    return pl.BlockSpec(memory_space=space)


def permute(value, shards, reps, shift, flip):
    route = [
        (s * reps + r, (s + shift) % shards * reps + (r ^ flip)) for s in range(shards) for r in range(reps)
    ]
    return lax.ppermute(value, AXES, route)


def exchange(held, bits, index, total):
    ways = 1 << len(bits)
    parts = [held]
    code = sum(((index >> bit) & 1) << i for i, bit in enumerate(bits))
    for k in range(1, ways):
        flip = sum(((k >> i) & 1) << bit for i, bit in enumerate(bits))
        parts.append(lax.ppermute(held, AXES, [(d, d ^ flip) for d in range(total)]))
    for i in range(len(bits)):
        swap = ((code >> i) & 1) == 1
        swapped = [parts[k ^ (1 << i)] for k in range(ways)]
        parts = [jnp.where(swap, b, a) for a, b in zip(parts, swapped)]
    return jnp.concatenate(parts, axis=0)


def local(shards, reps, entity, rel_weight, tile_rel, tile_head, tile_tail, tile_mask, negatives, tile_count):
    tiles = tile_rel.shape[0]
    block, width = entity.shape
    rels = rel_weight.shape[0]
    partition = block * reps
    smem, vmem = spec(pltpu.SMEM), spec(pltpu.VMEM)
    params = pltpu.CompilerParams(vmem_limit_bytes=min(8 * reps, 48) * MIB)

    tails = [permute(entity, shards, reps, 1, k) for k in reversed(range(reps))][::-1]
    others = [permute(entity, shards, reps, 0, k) for k in range(1, reps)]
    counts, weights, names, own = pl.pallas_call(
        prepare_kernel,
        out_shape=(
            jax.ShapeDtypeStruct((tiles, partition), F32),
            jax.ShapeDtypeStruct((tiles, width), F32),
            jax.ShapeDtypeStruct((1, LANES), F32),
            jax.ShapeDtypeStruct(entity.shape, F32),
        ),
        in_specs=[smem] + [spec(pl.ANY)] * 4,
        out_specs=(vmem, vmem, vmem, vmem),
        scratch_shapes=[
            pltpu.SMEM(tile_rel.shape, jnp.int32),
            pltpu.VMEM(negatives.shape, jnp.int32),
            pltpu.VMEM(rel_weight.shape, F32),
            pltpu.SemaphoreType.DMA((4,)),
        ],
        compiler_params=params,
        cost_estimate=pl.CostEstimate(flops=2 * tiles * partition * 256, bytes_accessed=4 << 20, transcendentals=0),
        name="prepare",
    )(tile_count, tile_rel, negatives, rel_weight, entity)
    mask = tile_mask.astype(F32)
    place = lax.axis_index("rep").astype(jnp.int32)[None]
    pieces = jax.ShapeDtypeStruct((reps, block, width), F32)
    coefficients = jax.ShapeDtypeStruct((tiles * block, partition), BF16)
    terms, head_parts, heads, grads_high, grads_low = pl.pallas_call(
        functools.partial(tiles_kernel, reps),
        out_shape=[jax.ShapeDtypeStruct((2 * tiles + SUBLANES, LANES), F32), pieces, pieces]
        + [coefficients] * 2,
        in_specs=[smem] * 2 + [spec(pl.ANY)] * 2 + [vmem] * (2 * reps + 4),
        out_specs=[vmem] * 5,
        scratch_shapes=[pltpu.VMEM((reps, block, width), F32)] * 2
        + [pltpu.SMEM((tiles,), jnp.int32)] * 2
        + [pltpu.SemaphoreType.DMA((2,))],
        compiler_params=params,
        cost_estimate=pl.CostEstimate(
            flops=12 * tiles * block * partition * width, bytes_accessed=4 << 20, transcendentals=0
        ),
        name="tiles",
    )(tile_count, place, tile_head, tile_tail, *tails[::-1], own, *others, mask, counts, weights, names)
    tail_parts = pl.pallas_call(
        tails_kernel,
        out_shape=pieces,
        in_specs=[smem, spec(pl.ANY)] + [vmem] * 4,
        out_specs=vmem,
        scratch_shapes=[
            pltpu.VMEM((reps, block, width), F32),
            pltpu.SMEM((tiles,), jnp.int32),
            pltpu.SemaphoreType.DMA,
        ],
        compiler_params=params,
        cost_estimate=pl.CostEstimate(
            flops=6 * tiles * block * partition * width, bytes_accessed=4 << 20, transcendentals=0
        ),
        name="tails",
    )(place, tile_head, heads, weights, grads_high, grads_low)

    total = shards * reps
    low = reps.bit_length() - 1
    top = total.bit_length() - 1
    order = list(range(top - 1, low, -1)) + list(range(low - 1, -1, -1))
    index = lax.axis_index("shard") * reps + lax.axis_index("rep")
    held = exchange(terms[None], order[:2], index, total)
    held, tail_parts = lax.optimization_barrier((held, tail_parts))
    returned = permute(tail_parts, shards, reps, -1, 0)
    for i in range(2, len(order), 2):
        held = exchange(held, order[i : i + 2], index, total)
    held, returned = lax.optimization_barrier((held, returned))
    theirs = lax.ppermute(held, AXES, [(d, d ^ (1 << low)) for d in range(total)])
    arrived = [permute(head_parts[k] + returned[k], shards, reps, 0, k) for k in range(1, reps)]
    half = combine(held, rels, width)
    rel_grad = combine(theirs, rels, width, half)
    entity_grad, _ = lax.optimization_barrier((head_parts[0] + returned[0], rel_grad))
    for part in arrived:
        entity_grad = entity_grad + part
    return (entity_grad, rel_grad)


def solution(mesh):
    sizes = dict(mesh.shape)
    return jax.shard_map(
        functools.partial(local, sizes["shard"], sizes["rep"]),
        mesh=mesh,
        in_specs=(
            P(AXES, None),
            P(),
            P(AXES),
            P(AXES),
            P(AXES),
            P(AXES, None, None),
            P(AXES, None),
            P(AXES),
        ),
        out_specs=(P(AXES, None), P()),
        check_vma=False,
    )
```

```python
import functools

import jax
import jax.numpy as jnp
from jax import lax
from jax.experimental import pallas as pl
from jax.experimental.pallas import tpu as pltpu
from jax.sharding import PartitionSpec as P

AXES = ("shard", "rep")
F32 = jnp.float32
BF16 = jnp.bfloat16
GROUP = 2
AHEAD = 1
LANES = 128
SUBLANES = 8
MIB = 1024 * 1024
LOG2E = 1.4426950408889634


def halves(value):
    high = value.astype(BF16)
    low = (value - high.astype(F32)).astype(BF16)
    return high, low


def stacked_left(pair, axis):
    return jnp.concatenate([pair[0], pair[0], pair[1]], axis=axis)


def stacked_right(pair, axis):
    return jnp.concatenate([pair[0], pair[1], pair[0]], axis=axis)


def dot(left, right, left_axis, right_axis):
    return lax.dot_general(
        left,
        right,
        dimension_numbers=(((left_axis,), (right_axis,)), ((), ())),
        preferred_element_type=F32,
    )


def prepare_kernel(count, rel_ids, negatives, rel_weight, entity, *refs):
    counts_out, weights_out, names_out, entity_out = refs[:4]
    ids, draws, table, sems = refs[4:]
    tiles, partition = counts_out.shape
    copies = [
        pltpu.make_async_copy(source, target, sems.at[i])
        for i, (source, target) in enumerate(
            [(rel_ids, ids), (negatives, draws), (rel_weight, table), (entity, entity_out)]
        )
    ]
    for copy in copies:
        copy.start()
    copies[1].wait()
    chosen = draws[...]
    columns = lax.broadcasted_iota(jnp.int32, (tiles, partition), 1)
    total = jnp.zeros((tiles, partition), F32)
    for draw in range(chosen.shape[1]):
        total = total + jnp.where(chosen[:, draw : draw + 1] == columns, 1.0, 0.0)
    slots = lax.broadcasted_iota(jnp.int32, (tiles, partition), 0)
    counts_out[...] = jnp.where(slots < count[0], total, 0.0)
    copies[0].wait()
    copies[2].wait()
    lanes = lax.broadcasted_iota(jnp.int32, (1, LANES), 1) % tiles
    names = jnp.zeros((1, LANES), jnp.int32)
    for tile in range(tiles):
        weights_out[tile : tile + 1, :] = table[pl.ds(ids[tile], 1), :]
        names = jnp.where(lanes == tile, ids[tile], names)
    names_out[...] = names.astype(F32)
    copies[3].wait()


def tiles_kernel(blocks, *refs):
    count, place, head_in_ids, tail_in_ids = refs[:4]
    tail_in = refs[4 : 4 + blocks][::-1]
    head_in = refs[4 + blocks : 4 + 2 * blocks]
    mask, counts, weights, names = refs[4 + 2 * blocks : 8 + 2 * blocks]
    terms = refs[8 + 2 * blocks]
    head_out, heads, grads_high, grads_low = refs[9 + 2 * blocks : 13 + 2 * blocks]
    tails, head_grad, head_ids, tail_ids, sems = refs[13 + 2 * blocks :]
    tiles, block, _ = mask.shape
    width = weights.shape[1]
    mine = place[0]
    copies = [
        pltpu.make_async_copy(head_in_ids, head_ids, sems.at[0]),
        pltpu.make_async_copy(tail_in_ids, tail_ids, sems.at[1]),
    ]
    for copy in copies:
        copy.start()
    for k in range(blocks):
        heads[mine ^ k] = head_in[k][...]
        tails[mine ^ k] = tail_in[k][...]
    head_grad[...] = jnp.zeros_like(head_grad)
    terms[2 * tiles :, :] = jnp.zeros((terms.shape[0] - 2 * tiles, LANES), F32)
    terms[2 * tiles : 2 * tiles + 1, :] = names[...]
    tail = tails[...].reshape(blocks * block, width)
    for_scores = stacked_right(halves(tail * -LOG2E), 1)
    for_mixed = stacked_right(halves(tail), 0)
    for copy in copies:
        copy.wait()

    def start(base):
        rows = [heads[head_ids[slot]] for slot in range(base, base + GROUP)]
        scales = [weights[slot : slot + 1, :] for slot in range(base, base + GROUP)]
        scaled = halves(jnp.concatenate([a * b for a, b in zip(rows, scales)], axis=0))
        return rows, scales, scaled, dot(stacked_left(scaled, 1), for_scores, 1, 1)

    def weigh(base, scores):
        grads = []
        for u, slot in enumerate(range(base, base + GROUP)):
            adjacent = mask[slot]
            live = slot < count[0]
            parts = []
            for b in range(blocks):
                flag = jnp.where(jnp.logical_and(live, tail_ids[slot] == b), 1.0, 0.0)
                times = counts[slot : slot + 1, b * block : (b + 1) * block]
                score = scores[u * block : (u + 1) * block, b * block : (b + 1) * block]
                odds = jnp.exp2(jnp.minimum(score, 115.0))
                parts.append((times - (adjacent * flag) * odds) / (1.0 + odds))
            grads.append(jnp.concatenate(parts, axis=1))
        return halves(jnp.concatenate(grads, axis=0))

    ahead = [start(base) for base in range(0, AHEAD * GROUP, GROUP)]
    for base in range(0, tiles, GROUP):
        if base + AHEAD * GROUP < tiles:
            ahead.append(start(base + AHEAD * GROUP))
        rows, scales, scaled, scores = ahead.pop(0)
        grads = weigh(base, scores)
        mixed = dot(stacked_left(grads, 1), for_mixed, 1, 0)
        for u, slot in enumerate(range(base, base + GROUP)):
            part = mixed[u * block : (u + 1) * block, :]
            term = jnp.sum(rows[u] * part, axis=0, keepdims=True)
            terms[slot : slot + 1, :] = term[:, :LANES]
            terms[tiles + slot : tiles + slot + 1, :] = term[:, LANES:]
            head_grad[head_ids[slot]] += part * scales[u]
        here = slice(base * block, (base + GROUP) * block)
        grads_high[here, :] = grads[0]
        grads_low[here, :] = grads[1]

    for k in range(blocks):
        head_out[k] = head_grad[mine ^ k]


def tails_kernel(place, head_in_ids, head_parts, heads, weights, grads_high, grads_low, *refs):
    pairs_out, (tail_grad, head_ids, sem) = refs[:-3], refs[-3:]
    blocks, block, _ = heads.shape
    tiles = weights.shape[0]
    copy = pltpu.make_async_copy(head_in_ids, head_ids, sem)
    copy.start()
    copy.wait()
    for base in range(0, tiles, GROUP):
        here = slice(base * block, (base + GROUP) * block)
        scaled = [heads[head_ids[slot]] * weights[slot : slot + 1, :] for slot in range(base, base + GROUP)]
        scaled = halves(jnp.concatenate(scaled, axis=0))
        grads = grads_high[here, :], grads_low[here, :]
        part = dot(stacked_left(grads, 0), stacked_right(scaled, 0), 0, 0).reshape(tail_grad.shape)
        if base == 0:
            tail_grad[...] = part
        else:
            tail_grad[...] += part
    for k in range(blocks):
        pairs_out[k][0] = head_parts[k]
        pairs_out[k][1] = tail_grad[place[0] ^ k]


def combine_kernel(gathered, before, out):
    devices = gathered.shape[0]
    tiles = (gathered.shape[1] - SUBLANES) // 2
    rels, width = out.shape
    padded = -(-rels // SUBLANES) * SUBLANES
    share = LANES // tiles
    lanes = lax.broadcasted_iota(jnp.int32, (1, LANES), 1) // tiles
    rows = lax.broadcasted_iota(jnp.int32, (padded, LANES), 0)
    hits = []
    for first in range(0, devices, share):
        names = gathered[first, 2 * tiles : 2 * tiles + 1, :]
        for other in range(1, share):
            names = jnp.where(lanes == other, gathered[first + other, 2 * tiles : 2 * tiles + 1, :], names)
        hits.append(jnp.where(rows == names.astype(jnp.int32), 1.0, 0.0).astype(BF16))
    hits = jnp.concatenate(hits, axis=1)
    left = gathered[:, :tiles, :].reshape(devices * tiles, LANES)
    right = gathered[:, tiles : 2 * tiles, :].reshape(devices * tiles, LANES)
    high, low = halves(jnp.concatenate([left, right], axis=1))
    total = jnp.dot(hits, high, preferred_element_type=F32) + jnp.dot(hits, low, preferred_element_type=F32)

    @pl.when(pl.program_id(0) == 0)
    def _():
        if before is None:
            out[...] = total[:rels]
        else:
            out[...] = before[...] + total[:rels]

    @pl.when(pl.program_id(0) != 0)
    def _():
        out[...] += total[:rels]


def combine(gathered, rels, width, before=None):
    batch = min(gathered.shape[0], 32)
    whole = pl.BlockSpec((rels, width), lambda i: (0, 0))
    kernel = combine_kernel
    operands, in_specs = [gathered], [pl.BlockSpec((batch,) + gathered.shape[1:], lambda i: (i, 0, 0))]
    if before is None:
        kernel = lambda held, out: combine_kernel(held, None, out)
    else:
        operands.append(before)
        in_specs.append(whole)
    return pl.pallas_call(
        kernel,
        out_shape=jax.ShapeDtypeStruct((rels, width), F32),
        grid=(gathered.shape[0] // batch,),
        in_specs=in_specs,
        out_specs=whole,
        compiler_params=pltpu.CompilerParams(vmem_limit_bytes=24 * MIB),
        cost_estimate=pl.CostEstimate(
            flops=4 * rels * gathered.shape[0] * 32 * width, bytes_accessed=2 << 20, transcendentals=0
        ),
        name="combine",
    )(*operands)


def spec(space):
    return pl.BlockSpec(memory_space=space)


def permute(value, shards, reps, shift, flip):
    route = [
        (s * reps + r, (s + shift) % shards * reps + (r ^ flip)) for s in range(shards) for r in range(reps)
    ]
    return lax.ppermute(value, AXES, route)


def exchange(held, bits, index, total):
    ways = 1 << len(bits)
    parts = [held]
    code = sum(((index >> bit) & 1) << i for i, bit in enumerate(bits))
    for k in range(1, ways):
        flip = sum(((k >> i) & 1) << bit for i, bit in enumerate(bits))
        parts.append(lax.ppermute(held, AXES, [(d, d ^ flip) for d in range(total)]))
    for i in range(len(bits)):
        swap = ((code >> i) & 1) == 1
        swapped = [parts[k ^ (1 << i)] for k in range(ways)]
        parts = [jnp.where(swap, b, a) for a, b in zip(parts, swapped)]
    return jnp.concatenate(parts, axis=0)


def local(shards, reps, entity, rel_weight, tile_rel, tile_head, tile_tail, tile_mask, negatives, tile_count):
    tiles = tile_rel.shape[0]
    block, width = entity.shape
    rels = rel_weight.shape[0]
    partition = block * reps
    smem, vmem = spec(pltpu.SMEM), spec(pltpu.VMEM)
    params = pltpu.CompilerParams(vmem_limit_bytes=min(8 * reps, 48) * MIB)

    tails = [permute(entity, shards, reps, 1, k) for k in reversed(range(reps))][::-1]
    others = [permute(entity, shards, reps, 0, k) for k in range(1, reps)]
    counts, weights, names, own = pl.pallas_call(
        prepare_kernel,
        out_shape=(
            jax.ShapeDtypeStruct((tiles, partition), F32),
            jax.ShapeDtypeStruct((tiles, width), F32),
            jax.ShapeDtypeStruct((1, LANES), F32),
            jax.ShapeDtypeStruct(entity.shape, F32),
        ),
        in_specs=[smem] + [spec(pl.ANY)] * 4,
        out_specs=(vmem, vmem, vmem, vmem),
        scratch_shapes=[
            pltpu.SMEM(tile_rel.shape, jnp.int32),
            pltpu.VMEM(negatives.shape, jnp.int32),
            pltpu.VMEM(rel_weight.shape, F32),
            pltpu.SemaphoreType.DMA((4,)),
        ],
        compiler_params=params,
        cost_estimate=pl.CostEstimate(flops=2 * tiles * partition * 256, bytes_accessed=4 << 20, transcendentals=0),
        name="prepare",
    )(tile_count, tile_rel, negatives, rel_weight, entity)
    mask = tile_mask.astype(F32)
    place = lax.axis_index("rep").astype(jnp.int32)[None]
    pieces = jax.ShapeDtypeStruct((reps, block, width), F32)
    coefficients = jax.ShapeDtypeStruct((tiles * block, partition), BF16)
    terms, head_parts, heads, grads_high, grads_low = pl.pallas_call(
        functools.partial(tiles_kernel, reps),
        out_shape=[jax.ShapeDtypeStruct((2 * tiles + SUBLANES, LANES), F32), pieces, pieces]
        + [coefficients] * 2,
        in_specs=[smem] * 2 + [spec(pl.ANY)] * 2 + [vmem] * (2 * reps + 4),
        out_specs=[vmem] * 5,
        scratch_shapes=[pltpu.VMEM((reps, block, width), F32)] * 2
        + [pltpu.SMEM((tiles,), jnp.int32)] * 2
        + [pltpu.SemaphoreType.DMA((2,))],
        compiler_params=params,
        cost_estimate=pl.CostEstimate(
            flops=12 * tiles * block * partition * width, bytes_accessed=4 << 20, transcendentals=0
        ),
        name="tiles",
    )(tile_count, place, tile_head, tile_tail, *tails[::-1], own, *others, mask, counts, weights, names)
    pairs = pl.pallas_call(
        tails_kernel,
        out_shape=[jax.ShapeDtypeStruct((2, block, width), F32)] * reps,
        in_specs=[smem, spec(pl.ANY)] + [vmem] * 5,
        out_specs=[vmem] * reps,
        scratch_shapes=[
            pltpu.VMEM((reps, block, width), F32),
            pltpu.SMEM((tiles,), jnp.int32),
            pltpu.SemaphoreType.DMA,
        ],
        compiler_params=params,
        cost_estimate=pl.CostEstimate(
            flops=6 * tiles * block * partition * width, bytes_accessed=4 << 20, transcendentals=0
        ),
        name="tails",
    )(place, tile_head, head_parts, heads, weights, grads_high, grads_low)

    total = shards * reps
    low = reps.bit_length() - 1
    top = total.bit_length() - 1
    order = [top - 1, *range(low - 1, -1, -1), *range(top - 2, low, -1)]
    index = lax.axis_index("shard") * reps + lax.axis_index("rep")
    held = exchange(terms[None], order[:2], index, total)
    held, pairs = lax.optimization_barrier((held, pairs))
    arrived = [permute(pairs[k], shards, reps, 0, k) for k in range(1, reps)]
    for i in range(2, len(order), 2):
        held = exchange(held, order[i : i + 2], index, total)
    held, arrived = lax.optimization_barrier((held, arrived))
    theirs = lax.ppermute(held, AXES, [(d, d ^ (1 << low)) for d in range(total)])
    summed = pairs[0]
    for part in arrived:
        summed = summed + part
    returned = permute(summed[1], shards, reps, -1, 0)
    half = combine(held, rels, width)
    rel_grad = combine(theirs, rels, width, half)
    entity_grad, _ = lax.optimization_barrier((summed[0], rel_grad))
    return (entity_grad + returned, rel_grad)


def solution(mesh):
    sizes = dict(mesh.shape)
    return jax.shard_map(
        functools.partial(local, sizes["shard"], sizes["rep"]),
        mesh=mesh,
        in_specs=(
            P(AXES, None),
            P(),
            P(AXES),
            P(AXES),
            P(AXES),
            P(AXES, None, None),
            P(AXES, None),
            P(AXES),
        ),
        out_specs=(P(AXES, None), P()),
        check_vma=False,
    )
```

```python
import functools

import jax
import jax.numpy as jnp
from jax import lax
from jax.experimental import pallas as pl
from jax.experimental.pallas import tpu as pltpu
from jax.sharding import PartitionSpec as P

AXES = ("shard", "rep")
F32 = jnp.float32
BF16 = jnp.bfloat16
GROUP = 2
AHEAD = 1
LANES = 128
SUBLANES = 8
MIB = 1024 * 1024
LOG2E = 1.4426950408889634


def halves(value):
    high = value.astype(BF16)
    low = (value - high.astype(F32)).astype(BF16)
    return high, low


def stacked_left(pair, axis):
    return jnp.concatenate([pair[0], pair[0], pair[1]], axis=axis)


def stacked_right(pair, axis):
    return jnp.concatenate([pair[0], pair[1], pair[0]], axis=axis)


def dot(left, right, left_axis, right_axis):
    return lax.dot_general(
        left,
        right,
        dimension_numbers=(((left_axis,), (right_axis,)), ((), ())),
        preferred_element_type=F32,
    )


def prepare_kernel(count, rel_ids, negatives, rel_weight, entity, *refs):
    counts_out, weights_out, names_out, entity_out = refs[:4]
    ids, draws, table, sems = refs[4:]
    tiles, partition = counts_out.shape
    copies = [
        pltpu.make_async_copy(source, target, sems.at[i])
        for i, (source, target) in enumerate(
            [(rel_ids, ids), (negatives, draws), (rel_weight, table), (entity, entity_out)]
        )
    ]
    for copy in copies:
        copy.start()
    copies[1].wait()
    chosen = draws[...]
    columns = lax.broadcasted_iota(jnp.int32, (tiles, partition), 1)
    total = jnp.zeros((tiles, partition), F32)
    for draw in range(chosen.shape[1]):
        total = total + jnp.where(chosen[:, draw : draw + 1] == columns, 1.0, 0.0)
    slots = lax.broadcasted_iota(jnp.int32, (tiles, partition), 0)
    counts_out[...] = jnp.where(slots < count[0], total, 0.0)
    copies[0].wait()
    copies[2].wait()
    lanes = lax.broadcasted_iota(jnp.int32, (1, LANES), 1) % tiles
    names = jnp.zeros((1, LANES), jnp.int32)
    for tile in range(tiles):
        weights_out[tile : tile + 1, :] = table[pl.ds(ids[tile], 1), :]
        names = jnp.where(lanes == tile, ids[tile], names)
    names_out[...] = names.astype(F32)
    copies[3].wait()


def tiles_kernel(blocks, *refs):
    count, place, head_in_ids, tail_in_ids = refs[:4]
    tail_in = refs[4 : 4 + blocks][::-1]
    head_in = refs[4 + blocks : 4 + 2 * blocks]
    mask, counts, weights, names = refs[4 + 2 * blocks : 8 + 2 * blocks]
    terms = refs[8 + 2 * blocks]
    head_out, heads, grads_high, grads_low = refs[9 + 2 * blocks : 13 + 2 * blocks]
    tails, head_grad, head_ids, tail_ids, sems = refs[13 + 2 * blocks :]
    tiles, block, _ = mask.shape
    width = weights.shape[1]
    mine = place[0]
    copies = [
        pltpu.make_async_copy(head_in_ids, head_ids, sems.at[0]),
        pltpu.make_async_copy(tail_in_ids, tail_ids, sems.at[1]),
    ]
    for copy in copies:
        copy.start()
    for k in range(blocks):
        heads[mine ^ k] = head_in[k][...]
        tails[mine ^ k] = tail_in[k][...]
    head_grad[...] = jnp.zeros_like(head_grad)
    terms[2 * tiles :, :] = jnp.zeros((terms.shape[0] - 2 * tiles, LANES), F32)
    terms[2 * tiles : 2 * tiles + 1, :] = names[...]
    tail = tails[...].reshape(blocks * block, width)
    for_scores = stacked_right(halves(tail * -LOG2E), 1)
    for_mixed = stacked_right(halves(tail), 0)
    for copy in copies:
        copy.wait()

    def start(base):
        rows = [heads[head_ids[slot]] for slot in range(base, base + GROUP)]
        scales = [weights[slot : slot + 1, :] for slot in range(base, base + GROUP)]
        scaled = halves(jnp.concatenate([a * b for a, b in zip(rows, scales)], axis=0))
        return rows, scales, scaled, dot(stacked_left(scaled, 1), for_scores, 1, 1)

    def weigh(base, scores):
        grads = []
        for u, slot in enumerate(range(base, base + GROUP)):
            adjacent = mask[slot]
            live = slot < count[0]
            parts = []
            for b in range(blocks):
                flag = jnp.where(jnp.logical_and(live, tail_ids[slot] == b), 1.0, 0.0)
                times = counts[slot : slot + 1, b * block : (b + 1) * block]
                score = scores[u * block : (u + 1) * block, b * block : (b + 1) * block]
                odds = jnp.exp2(jnp.minimum(score, 115.0))
                parts.append((times - (adjacent * flag) * odds) / (1.0 + odds))
            grads.append(jnp.concatenate(parts, axis=1))
        return halves(jnp.concatenate(grads, axis=0))

    ahead = [start(base) for base in range(0, AHEAD * GROUP, GROUP)]
    for base in range(0, tiles, GROUP):
        if base + AHEAD * GROUP < tiles:
            ahead.append(start(base + AHEAD * GROUP))
        rows, scales, scaled, scores = ahead.pop(0)
        grads = weigh(base, scores)
        mixed = dot(stacked_left(grads, 1), for_mixed, 1, 0)
        for u, slot in enumerate(range(base, base + GROUP)):
            part = mixed[u * block : (u + 1) * block, :]
            term = jnp.sum(rows[u] * part, axis=0, keepdims=True)
            terms[slot : slot + 1, :] = term[:, :LANES]
            terms[tiles + slot : tiles + slot + 1, :] = term[:, LANES:]
            head_grad[head_ids[slot]] += part * scales[u]
        here = slice(base * block, (base + GROUP) * block)
        grads_high[here, :] = grads[0]
        grads_low[here, :] = grads[1]

    for k in range(blocks):
        head_out[k] = head_grad[mine ^ k]


def tails_kernel(place, head_in_ids, head_parts, heads, weights, grads_high, grads_low, *refs):
    pairs_out, (tail_grad, head_ids, sem) = refs[:-3], refs[-3:]
    blocks, block, _ = heads.shape
    tiles = weights.shape[0]
    copy = pltpu.make_async_copy(head_in_ids, head_ids, sem)
    copy.start()
    copy.wait()
    for base in range(0, tiles, GROUP):
        here = slice(base * block, (base + GROUP) * block)
        scaled = [heads[head_ids[slot]] * weights[slot : slot + 1, :] for slot in range(base, base + GROUP)]
        scaled = halves(jnp.concatenate(scaled, axis=0))
        grads = grads_high[here, :], grads_low[here, :]
        part = dot(stacked_left(grads, 0), stacked_right(scaled, 0), 0, 0).reshape(tail_grad.shape)
        if base == 0:
            tail_grad[...] = part
        else:
            tail_grad[...] += part
    for k in range(blocks):
        pairs_out[k][0] = head_parts[k]
        pairs_out[k][1] = tail_grad[place[0] ^ k]


def combine_kernel(gathered, before, out):
    devices = gathered.shape[0]
    tiles = (gathered.shape[1] - SUBLANES) // 2
    rels, width = out.shape
    padded = -(-rels // SUBLANES) * SUBLANES
    share = LANES // tiles
    lanes = lax.broadcasted_iota(jnp.int32, (1, LANES), 1) // tiles
    rows = lax.broadcasted_iota(jnp.int32, (padded, LANES), 0)
    hits = []
    for first in range(0, devices, share):
        names = gathered[first, 2 * tiles : 2 * tiles + 1, :]
        for other in range(1, share):
            names = jnp.where(lanes == other, gathered[first + other, 2 * tiles : 2 * tiles + 1, :], names)
        hits.append(jnp.where(rows == names.astype(jnp.int32), 1.0, 0.0).astype(BF16))
    hits = jnp.concatenate(hits, axis=1)
    left = gathered[:, :tiles, :].reshape(devices * tiles, LANES)
    right = gathered[:, tiles : 2 * tiles, :].reshape(devices * tiles, LANES)
    high, low = halves(jnp.concatenate([left, right], axis=1))
    total = jnp.dot(hits, high, preferred_element_type=F32) + jnp.dot(hits, low, preferred_element_type=F32)

    @pl.when(pl.program_id(0) == 0)
    def _():
        if before is None:
            out[...] = total[:rels]
        else:
            out[...] = before[...] + total[:rels]

    @pl.when(pl.program_id(0) != 0)
    def _():
        out[...] += total[:rels]


def combine(gathered, rels, width, before=None):
    batch = min(gathered.shape[0], 32)
    whole = pl.BlockSpec((rels, width), lambda i: (0, 0))
    kernel = combine_kernel
    operands, in_specs = [gathered], [pl.BlockSpec((batch,) + gathered.shape[1:], lambda i: (i, 0, 0))]
    if before is None:
        kernel = lambda held, out: combine_kernel(held, None, out)
    else:
        operands.append(before)
        in_specs.append(whole)
    return pl.pallas_call(
        kernel,
        out_shape=jax.ShapeDtypeStruct((rels, width), F32),
        grid=(gathered.shape[0] // batch,),
        in_specs=in_specs,
        out_specs=whole,
        compiler_params=pltpu.CompilerParams(vmem_limit_bytes=24 * MIB),
        cost_estimate=pl.CostEstimate(
            flops=4 * rels * gathered.shape[0] * 32 * width, bytes_accessed=2 << 20, transcendentals=0
        ),
        name="combine",
    )(*operands)


def spec(space):
    return pl.BlockSpec(memory_space=space)


def permute(value, shards, reps, shift, flip):
    route = [
        (s * reps + r, (s + shift) % shards * reps + (r ^ flip)) for s in range(shards) for r in range(reps)
    ]
    return lax.ppermute(value, AXES, route)


def exchange(held, bits, index, total):
    ways = 1 << len(bits)
    parts = [held]
    code = sum(((index >> bit) & 1) << i for i, bit in enumerate(bits))
    for k in range(1, ways):
        flip = sum(((k >> i) & 1) << bit for i, bit in enumerate(bits))
        parts.append(lax.ppermute(held, AXES, [(d, d ^ flip) for d in range(total)]))
    for i in range(len(bits)):
        swap = ((code >> i) & 1) == 1
        swapped = [parts[k ^ (1 << i)] for k in range(ways)]
        parts = [jnp.where(swap, b, a) for a, b in zip(parts, swapped)]
    return jnp.concatenate(parts, axis=0)


def local(shards, reps, entity, rel_weight, tile_rel, tile_head, tile_tail, tile_mask, negatives, tile_count):
    tiles = tile_rel.shape[0]
    block, width = entity.shape
    rels = rel_weight.shape[0]
    partition = block * reps
    smem, vmem = spec(pltpu.SMEM), spec(pltpu.VMEM)
    params = pltpu.CompilerParams(vmem_limit_bytes=min(8 * reps, 48) * MIB)

    tails = [permute(entity, shards, reps, 1, k) for k in reversed(range(reps))][::-1]
    others = [permute(entity, shards, reps, 0, k) for k in range(1, reps)]
    counts, weights, names, own = pl.pallas_call(
        prepare_kernel,
        out_shape=(
            jax.ShapeDtypeStruct((tiles, partition), F32),
            jax.ShapeDtypeStruct((tiles, width), F32),
            jax.ShapeDtypeStruct((1, LANES), F32),
            jax.ShapeDtypeStruct(entity.shape, F32),
        ),
        in_specs=[smem] + [spec(pl.ANY)] * 4,
        out_specs=(vmem, vmem, vmem, vmem),
        scratch_shapes=[
            pltpu.SMEM(tile_rel.shape, jnp.int32),
            pltpu.VMEM(negatives.shape, jnp.int32),
            pltpu.VMEM(rel_weight.shape, F32),
            pltpu.SemaphoreType.DMA((4,)),
        ],
        compiler_params=params,
        cost_estimate=pl.CostEstimate(flops=2 * tiles * partition * 256, bytes_accessed=4 << 20, transcendentals=0),
        name="prepare",
    )(tile_count, tile_rel, negatives, rel_weight, entity)
    mask = tile_mask.astype(F32)
    place = lax.axis_index("rep").astype(jnp.int32)[None]
    pieces = jax.ShapeDtypeStruct((reps, block, width), F32)
    coefficients = jax.ShapeDtypeStruct((tiles * block, partition), BF16)
    terms, head_parts, heads, grads_high, grads_low = pl.pallas_call(
        functools.partial(tiles_kernel, reps),
        out_shape=[jax.ShapeDtypeStruct((2 * tiles + SUBLANES, LANES), F32), pieces, pieces]
        + [coefficients] * 2,
        in_specs=[smem] * 2 + [spec(pl.ANY)] * 2 + [vmem] * (2 * reps + 4),
        out_specs=[vmem] * 5,
        scratch_shapes=[pltpu.VMEM((reps, block, width), F32)] * 2
        + [pltpu.SMEM((tiles,), jnp.int32)] * 2
        + [pltpu.SemaphoreType.DMA((2,))],
        compiler_params=params,
        cost_estimate=pl.CostEstimate(
            flops=12 * tiles * block * partition * width, bytes_accessed=4 << 20, transcendentals=0
        ),
        name="tiles",
    )(tile_count, place, tile_head, tile_tail, *tails[::-1], own, *others, mask, counts, weights, names)
    pairs = pl.pallas_call(
        tails_kernel,
        out_shape=[jax.ShapeDtypeStruct((2, block, width), F32)] * reps,
        in_specs=[smem, spec(pl.ANY)] + [vmem] * 5,
        out_specs=[vmem] * reps,
        scratch_shapes=[
            pltpu.VMEM((reps, block, width), F32),
            pltpu.SMEM((tiles,), jnp.int32),
            pltpu.SemaphoreType.DMA,
        ],
        compiler_params=params,
        cost_estimate=pl.CostEstimate(
            flops=6 * tiles * block * partition * width, bytes_accessed=4 << 20, transcendentals=0
        ),
        name="tails",
    )(place, tile_head, head_parts, heads, weights, grads_high, grads_low)

    total = shards * reps
    low = reps.bit_length() - 1
    top = total.bit_length() - 1
    order = [top - 1, *range(low - 1, -1, -1), *range(top - 2, low, -1)]
    index = lax.axis_index("shard") * reps + lax.axis_index("rep")
    held = exchange(terms[None], order[:2], index, total)
    held, pairs = lax.optimization_barrier((held, pairs))
    arrived = [permute(pairs[k], shards, reps, 0, k) for k in range(1, reps)]
    for i in range(2, len(order), 2):
        held = exchange(held, order[i : i + 2][::-1], index, total)
    held, arrived = lax.optimization_barrier((held, arrived))
    theirs = lax.ppermute(held, AXES, [(d, d ^ (1 << low)) for d in range(total)])
    summed = pairs[0]
    for part in arrived:
        summed = summed + part
    returned = permute(summed[1], shards, reps, -1, 0)
    half = combine(held, rels, width)
    rel_grad = combine(theirs, rels, width, half)
    entity_grad, _ = lax.optimization_barrier((summed[0], rel_grad))
    return (entity_grad + returned, rel_grad)


def solution(mesh):
    sizes = dict(mesh.shape)
    return jax.shard_map(
        functools.partial(local, sizes["shard"], sizes["rep"]),
        mesh=mesh,
        in_specs=(
            P(AXES, None),
            P(),
            P(AXES),
            P(AXES),
            P(AXES),
            P(AXES, None, None),
            P(AXES, None),
            P(AXES),
        ),
        out_specs=(P(AXES, None), P()),
        check_vma=False,
    )
```
